256 devices in a mesh: segment: 2 (over core), space: 32 (over z, x), dp: 4 (over y).
Axes of the slice: x: 4, y: 4, z: 8, core: 2. Of those that a mesh axis runs over, the one named last changes fastest.
Arguments:
- latents: bfloat16 [8, 1, 128, 128, 320], P('dp', None, 'space'), may hold values from -14 to 14
- hint: bfloat16 [8, 1, 128, 128, 320], P('dp', None, 'space'), may hold values from -6 to 6
- cotangent: bfloat16 [8, 1, 128, 128, 320], P('dp', None, 'space'), may hold values from -6 to 6
- conv_weight: bfloat16 [2, 9, 640, 320], P('segment'), may hold values from -0.078125 to 0.078125
- ctrl_weight: bfloat16 [2, 320, 320], P('segment'), may hold values from -0.3125 to 0.3125
- norm_gain: float32 [2, 640], P('segment'), may hold values from 0.1 to 1.9
- norm_bias: float32 [2, 640], P('segment'), may hold values from -3 to 3
Outputs:
- acts: bfloat16 [2, 8, 1, 128, 128, 320], P('segment', 'dp', None, 'space')
- grad_conv: bfloat16 [2, 9, 640, 320], P('segment')
- grad_ctrl: float32 [2, 320, 320], P('segment')
- grad_gain: float32 [2, 640], P('segment')
- grad_bias: float32 [2, 640], P('segment')
The draws below stay inside these ranges and needn't reach their ends.
All inputs are finite; a program needn't handle non-finite values.
Results may differ from the reference program's by a relative error of at most 0.0061.
Values may be sent and summed in bfloat16 or wider, within the bound.
A program may use at most 128 MiB of HBM per device.

```python
import jax
import jax.numpy as jnp
from jax import lax

C = 320
GROUPS = 32
WCOL = 128
FRAMES = 1
H = 128
BATCH = 8
N_SEGMENT = 2


def draw_latents(key, part):
    base_key, chan_key = jax.random.split(jax.random.fold_in(key, 11))
    shape = (BATCH, FRAMES, H, WCOL, C)
    position = jnp.arange(H, dtype=jnp.float32) / max(H - 1, 1)
    row_scale = 10.0 ** (0.6 * position - 0.3)
    chan_scale = jnp.exp(jax.random.uniform(chan_key, (C,), jnp.float32, -0.5, 0.5))
    base = jnp.clip(jax.random.normal(base_key, shape, jnp.float32), -4.0, 4.0)
    values = base * row_scale[None, None, :, None, None] * chan_scale
    return values.astype(jnp.bfloat16)


def block_scale(stream_key, shape, cuts, smallest, top_value):
    def one(dim, blocks):
        heights = jax.random.uniform(jax.random.fold_in(jax.random.fold_in(stream_key, 6), dim), (blocks,), jnp.float32, smallest / len(cuts), top_value / len(cuts))
        return jnp.repeat(jnp.exp(heights), shape[dim] // blocks).reshape((-1,) + (1,) * (len(shape) - dim - 1))

    gain = one(*cuts[0])
    for cut in cuts[1:]:
        gain = gain * one(*cut)
    return gain


def noise(own_key, shape, spread, bound, pieces=(), kind=jnp.bfloat16):
    loudness = block_scale(own_key, shape, pieces, -0.22, 0.18) if pieces else 1.0
    array = jax.random.normal(own_key, shape, jnp.float32) * spread * loudness
    return jnp.minimum(jnp.maximum(array, -bound), bound).astype(kind)


def setup_inputs(seed: int = 0) -> dict:
    seeds = jax.random.split(jax.random.key(seed), 8)
    return {
        "latents": draw_latents(jax.random.fold_in(seeds[7], 71), 0),
        "hint": noise(seeds[1], (BATCH, FRAMES, H, WCOL, C), 1.0, 6.0, ((0, 4), (2, 32))),
        "cotangent": noise(seeds[2], (BATCH, FRAMES, H, WCOL, C), 1.0, 6.0, ((0, 4), (2, 32))),
        "conv_weight": noise(seeds[3], (N_SEGMENT, 9, 2 * C, C), (18 * C) ** -0.5, 0.078125, ((0, 2),)),
        "ctrl_weight": noise(seeds[4], (N_SEGMENT, C, C), C ** -0.5, 0.3125, ((0, 2),)),
        "norm_gain": jnp.clip(1.0 + 0.18 * jax.random.normal(seeds[5], (N_SEGMENT, 2 * C), jnp.float32), 0.1, 1.9),
        "norm_bias": noise(seeds[6], (N_SEGMENT, 2 * C), 0.5, 3.0, ((0, 2),), jnp.float32),
    }


epsilon = 1e-05

def group_mean(values, groups):
    shaped = values.reshape(values.shape[:-1] + (groups, values.shape[-1] // groups))
    means = lax.optimization_barrier(jnp.mean(shaped, axis=(1, 2, 4), keepdims=True))
    return jnp.broadcast_to(means, shaped.shape).reshape(values.shape)

def convolve(padded, weight, row_count, col_count):
    width = padded.shape[-1]
    total = jnp.zeros((padded.shape[0] * row_count * col_count, weight.shape[-1]), jnp.float32)
    for tap_id in range(9):
        row_off, col_off = divmod(tap_id, 3)
        piece = padded[:, row_off:row_off + row_count, col_off:col_off + col_count, :].reshape(-1, width)
        total = total + jnp.dot(piece, weight[tap_id], preferred_element_type=jnp.float32)
    return total.reshape(padded.shape[0], row_count, col_count, -1)

def transpose_conv(source, weight, row_count, col_count):
    channels = source.shape[-1]
    total = jnp.zeros((source.shape[0] * row_count * col_count, weight.shape[1]), jnp.float32)
    for tap_id in range(9):
        row_off, col_off = divmod(tap_id, 3)
        piece = source[:, 2 - row_off:2 - row_off + row_count, 2 - col_off:2 - col_off + col_count, :].reshape(-1, channels)
        total = total + lax.dot_general(piece, weight[tap_id], (((1,), (1,)), ((), ())), preferred_element_type=jnp.float32)
    return total.reshape(source.shape[0], row_count, col_count, -1)

def weight_grad(padded, grad_out, row_count, col_count):
    width = padded.shape[-1]
    flat = grad_out.reshape(-1, grad_out.shape[-1])
    parts = []
    for tap_id in range(9):
        row_off, col_off = divmod(tap_id, 3)
        piece = padded[:, row_off:row_off + row_count, col_off:col_off + col_count, :].reshape(-1, width)
        parts.append(lax.dot_general(piece, flat, (((0,), (0,)), ((), ())), preferred_element_type=jnp.float32))
    return jnp.stack(parts)

def segment_forward(current, skip, hint_one, weight, control, gain_vec, bias_vec):
    if skip is None:
        joined = current
    else:
        joined = jnp.concatenate([current, skip], -1)
    width = joined.shape[-1]
    frames, row_count, col_count, channels = current.shape
    values = joined.astype(jnp.float32)
    centered = values - group_mean(values, GROUPS)
    rstd = lax.rsqrt(group_mean(centered * centered, GROUPS) + epsilon)
    normed = centered * rstd
    raised = normed * gain_vec[:width] + bias_vec[:width]
    act = jax.nn.silu(raised).astype(jnp.bfloat16)
    padded = jnp.pad(act, ((0, 0), (1, 1), (1, 1), (0, 0)))
    mixed = convolve(padded, weight[:, :width], row_count, col_count)
    ctrl = jnp.dot(hint_one.reshape(-1, channels), control, preferred_element_type=jnp.float32).reshape(mixed.shape)
    output = (current.astype(jnp.float32) + mixed + ctrl).astype(jnp.bfloat16)
    return (output, (padded, normed, raised, rstd))

def segment_backward(grad_out, saved, hint_one, weight, gain_vec):
    padded, normed, raised, rstd = saved
    frames, row_count, col_count, channels = grad_out.shape
    width = padded.shape[-1]
    flat = grad_out.reshape(-1, channels)
    ctrl_part = lax.dot_general(hint_one.reshape(-1, channels), flat, (((0,), (0,)), ((), ())), preferred_element_type=jnp.float32)
    kernel_part = weight_grad(padded, grad_out, row_count, col_count)
    grad_pad = jnp.pad(grad_out, ((0, 0), (1, 1), (1, 1), (0, 0)))
    dact = transpose_conv(grad_pad, weight[:, :width], row_count, col_count)
    sigma = jax.nn.sigmoid(raised)
    draised = dact * sigma * (1.0 + raised * (1.0 - sigma))
    gain_part = lax.optimization_barrier(jnp.sum(draised * normed, axis=(0, 1, 2)))
    bias_part = lax.optimization_barrier(jnp.sum(draised, axis=(0, 1, 2)))
    dnormed = draised * gain_vec[:width]
    djoined = rstd * (dnormed - group_mean(dnormed, GROUPS) - normed * group_mean(dnormed * normed, GROUPS))
    back_grad = (grad_out.astype(jnp.float32) + djoined[..., :channels]).astype(jnp.bfloat16)
    side_grad = djoined[..., channels:].astype(jnp.bfloat16)
    return (back_grad, side_grad, kernel_part, ctrl_part, gain_part, bias_part)

def widen(values, total, axis):
    extra = total - values.shape[axis]
    if extra == 0:
        return values
    pads = [(0, 0)] * values.ndim
    pads[axis] = (0, extra)
    return jnp.pad(values, pads)

def reference(latents, hint, cotangent, conv_weight, ctrl_weight, norm_gain, norm_bias):
    segments = conv_weight.shape[0]
    halfway = segments // 2
    wide_ch = conv_weight.shape[2]

    def one_sample(carry, inputs):
        first, hint_one, grad_last = inputs
        outputs = []
        saved = []
        current = first
        for segment_id in range(segments):
            skip = None if segment_id < halfway else outputs[segment_id - halfway]
            current, kept = segment_forward(current, skip, hint_one, conv_weight[segment_id], ctrl_weight[segment_id], norm_gain[segment_id], norm_bias[segment_id])
            outputs.append(current)
            saved.append(kept)
        kernel_list = [None] * segments
        ctrl_list = [None] * segments
        gain_list = [None] * segments
        bias_list = [None] * segments
        side_grads = [None] * segments
        back_grad = None
        for segment_id in reversed(range(segments)):
            if segment_id == segments - 1:
                grad_out = grad_last
            elif segment_id >= halfway:
                grad_out = back_grad
            else:
                grad_out = (back_grad.astype(jnp.float32) + side_grads[segment_id + halfway].astype(jnp.float32)).astype(jnp.bfloat16)
            back_grad, side_grad, kernel_part, ctrl_part, gain_part, bias_part = segment_backward(grad_out, saved[segment_id], hint_one, conv_weight[segment_id], norm_gain[segment_id])
            side_grads[segment_id] = side_grad
            kernel_list[segment_id] = widen(kernel_part, wide_ch, 1)
            ctrl_list[segment_id] = ctrl_part
            gain_list[segment_id] = widen(gain_part, wide_ch, 0)
            bias_list[segment_id] = widen(bias_part, wide_ch, 0)
        kernel_acc, ctrl_acc, gain_acc, bias_acc = carry
        carry = (kernel_acc + jnp.stack(kernel_list), ctrl_acc + jnp.stack(ctrl_list), gain_acc + jnp.stack(gain_list), bias_acc + jnp.stack(bias_list))
        return (carry, jnp.stack(outputs))
    start = (jnp.zeros(conv_weight.shape, jnp.float32), jnp.zeros(ctrl_weight.shape, jnp.float32), jnp.zeros(norm_gain.shape, jnp.float32), jnp.zeros(norm_bias.shape, jnp.float32))
    totals, stacked = lax.scan(one_sample, start, (latents, hint, cotangent))
    acts = jnp.moveaxis(stacked, 0, 1)
    return (acts, totals[0].astype(jnp.bfloat16), totals[1], totals[2], totals[3])
```

```python
import functools

import jax
import jax.numpy as jnp
from jax import lax
from jax.experimental import pallas as pl
from jax.experimental.pallas import tpu as pltpu
from jax.sharding import PartitionSpec as P

MESH = pl.DeviceIdType.MESH
F32 = jnp.float32
BF16 = jnp.bfloat16
EPS = 1e-05
GROUPS = 32
PART = 2048
ROW = 128
CHUNK = 32


def nt_dot(a, b):
    return lax.dot_general(a, b, (((1,), (1,)), ((), ())), preferred_element_type=F32)


def tn_dot(a, b):
    return lax.dot_general(a, b, (((0,), (0,)), ((), ())), preferred_element_type=F32)


def nn_dot(a, b):
    return jnp.dot(a, b, preferred_element_type=F32)


def fold(v):
    return v.reshape(v.shape[0] // 8, 8, v.shape[1]).sum(axis=0)


def sigmoid(v):
    return 1.0 / (1.0 + jnp.exp(-v))


class Slots:
    def __init__(self):
        self.index = {}

    def __call__(self, name):
        return self.index.setdefault(name, len(self.index))


def body(
    dims,
    slots,
    lat_hbm, hint_hbm, cot_hbm, w_hbm, cw_hbm, gain_ref, bias_ref,
    acts_hbm, conv_out, ctrl_out, gain_out, bias_out,
    x_ext, g_ext, hint_v, w_v, cw_v, act, y, dact, shifted, out_v,
    s_send, s_recv, stat_v, grads, r1, r2, r3, s1, s2, gathered, zeros_v, ctrl_v,
    send_sem, recv_sem, local_sem,
):
    NZ, NX, NY, samples, rows, channels = dims
    cells = rows * ROW
    ext = cells + 2 * ROW
    space_count = NZ * NX
    seg = lax.axis_index("segment")
    space = lax.axis_index("space")
    dp = lax.axis_index("dp")
    zi = space // NX
    xi = lax.rem(space, NX)
    other = 1 - seg
    up = lax.rem(space + space_count - 1, space_count)
    down = lax.rem(space + 1, space_count)
    size = {"x": NX, "y": NY, "z": NZ}
    mine = {"x": xi, "y": dp, "z": zi}

    def peer(axis, k, core=None):
        if axis == "x":
            place = {"space": zi * NX + lax.rem(xi + k, NX), "dp": dp}
        elif axis == "z":
            place = {"space": lax.rem(zi + k, NZ) * NX + xi, "dp": dp}
        else:
            place = {"space": space, "dp": lax.rem(dp + k, NY)}
        place["segment"] = seg if core is None else core
        return place

    def at(space_id, core):
        return {"space": space_id, "dp": dp, "segment": core}

    def send(name, src, dst, place):
        slot = slots(name)
        return pltpu.make_async_remote_copy(
            src_ref=src, dst_ref=dst, send_sem=send_sem.at[slot], recv_sem=recv_sem.at[slot],
            device_id=(place["segment"], place["space"], place["dp"]), device_id_type=MESH,
        )

    def local(name, src, dst):
        return pltpu.make_async_copy(src, dst, local_sem.at[slots("local " + name)])

    inner = pl.ds(ROW, cells)
    low, high = pl.ds(0, ROW), pl.ds(ROW + cells, ROW)
    first, last = pl.ds(ROW, ROW), pl.ds(cells, ROW)
    kernel_rows = 9 * channels

    def loads(is_encoder):
        table = {
            "hint": (hint_hbm, hint_v),
            "weight": (w_hbm, w_v),
            "control": (cw_hbm, cw_v),
        }
        if is_encoder:
            table["main"] = (lat_hbm, x_ext.at[:, inner, :])
        else:
            table["main"] = (cot_hbm, g_ext.at[:, inner, :])
        return {key: functools.partial(local, key, *pair) for key, pair in table.items()}

    @pl.when(seg == 0)
    def _():
        for key in ("main", "control", "hint", "weight"):
            loads(True)[key]().start()

    @pl.when(seg == 1)
    def _():
        for key in ("main", "hint", "weight", "control"):
            loads(False)[key]().start()

    barrier = pltpu.get_barrier_semaphore()
    places = [peer("x", k) for k in range(1, NX)]
    places += [peer("y", k) for k in range(1, NY)]
    places += [peer("z", k) for k in range(1, NZ)]
    places += [peer("z", k, other) for k in range(NZ)]
    places += [at(n, c) for n in (up, down) for c in (seg, other)]
    for place in places:
        pl.semaphore_signal(
            barrier, inc=1,
            device_id=(place["segment"], place["space"], place["dp"]), device_id_type=MESH,
        )
    pl.semaphore_wait(barrier, len(places))

    lane = lax.broadcasted_iota(jnp.int32, (channels, channels), 0).astype(F32)
    lane_t = lax.broadcasted_iota(jnp.int32, (channels, channels), 1).astype(F32)

    def group_mean(values, width):
        same = jnp.floor((lane + 0.5) / width) == jnp.floor((lane_t + 0.5) / width)
        return jnp.dot(
            values, jnp.where(same, 1.0, 0.0),
            precision=lax.Precision.HIGHEST, preferred_element_type=F32,
        ) / width

    def edges(halo_name, ref, src, core):
        return [
            send(halo_name + " down", src[1], ref.at[:, low, :], at(down, core)),
            send(halo_name + " up", src[0], ref.at[:, high, :], at(up, core)),
        ]

    def zero_outside(ref):
        blank = jnp.zeros((samples, ROW, channels), ref.dtype)

        @pl.when(space == 0)
        def _():
            ref[:, 0:ROW, :] = blank

        @pl.when(space == space_count - 1)
        def _():
            ref[:, ROW + cells:ext, :] = blank

    def local_stats(ref, base, name):
        for b in range(samples):
            def add(i, total):
                v = ref[b, pl.ds(pl.multiple_of(base + i * CHUNK, CHUNK), CHUNK), :].astype(F32)
                return total + fold(v)
            total = lax.fori_loop(0, cells // CHUNK, add, jnp.zeros((8, channels), F32))
            mean = total.sum(axis=0, keepdims=True) / cells

            def square(i, total):
                v = ref[b, pl.ds(pl.multiple_of(base + i * CHUNK, CHUNK), CHUNK), :].astype(F32) - mean
                return total + fold(v * v)
            spread = lax.fori_loop(0, cells // CHUNK, square, jnp.zeros((8, channels), F32))
            s_send[slots.buffer(name), b:b + 1, :] = mean
            s_send[slots.buffer(name), samples + b:samples + b + 1, :] = spread.sum(axis=0, keepdims=True)

    def exchange(name, axis, core=None, own=True):
        src = s_send.at[slots.buffer(name)]
        copies = []
        for k in range(0 if core is not None else 1, size[axis]):
            label = f"{name} {k}"
            copies.append(send(label, src, s_recv.at[slots.inbox(label)], peer(axis, k, core)))
        return copies

    def arrivals(name, axis, own):
        out = []
        if own:
            out.append(s_send.at[slots.buffer(name)])
        for k in range(1 if own else 0, size[axis]):
            out.append(s_recv.at[slots.inbox(f"{name} {k}")])
        return out

    def merge(refs, count):
        mean = sum(r[0:samples, :] for r in refs) / len(refs)
        spread = sum(r[samples:2 * samples, :] for r in refs)
        apart = sum(jnp.square(r[0:samples, :] - mean) for r in refs)
        return mean, spread + count * apart

    def finish_stats(mean, spread, width):
        total = cells * space_count
        padded = jnp.concatenate([mean, jnp.zeros((8 - samples, channels), F32)], axis=0)
        middle = group_mean(padded, width)
        offset = padded - middle
        both = jnp.concatenate([spread, jnp.zeros((8 - samples, channels), F32)], axis=0)
        var = group_mean(both / total + offset * offset, width)
        stat_v[0] = middle
        stat_v[1] = lax.rsqrt(var + EPS)

    def small_sum(name, axes, value):
        for axis in axes:
            step = f"{name} {axis}"
            s_send[slots.buffer(step)] = value
            copies = exchange(step, axis)
            for c in copies:
                c.start()
            for c in copies:
                c.wait()
            value = sum(r[...] for r in arrivals(step, axis, True))
        return value

    def activate(halves):
        for b in range(samples):
            middle = stat_v[0, b:b + 1, :]
            scale = stat_v[1, b:b + 1, :]

            def step(i, carry):
                where = pl.ds(pl.multiple_of(i * CHUNK, CHUNK), CHUNK)
                xhat = (x_ext[b, where, :].astype(F32) - middle) * scale
                for h in halves:
                    u = xhat * gain_ref[h:h + 1, :] + bias_ref[h:h + 1, :]
                    act[h, b, where, :] = (u * sigmoid(u)).astype(BF16)
                return carry
            lax.fori_loop(0, ext // CHUNK, step, 0)
        for h in halves:
            zero_outside(act.at[h])

    def column_mask(shape, column):
        return lax.broadcasted_iota(jnp.int32, shape, 0) != column

    def shift(v, step):
        column = 0 if step == 1 else ROW - 1
        moved = pltpu.roll(v, step % ROW, axis=0)
        return jnp.where(column_mask(v.shape, column), moved, 0.0)

    BLOCK = 2 * ROW

    def forward(halves):
        def step(i, carry):
            b = i // (cells // BLOCK)
            start = pl.multiple_of(lax.rem(i, cells // BLOCK) * BLOCK, BLOCK)
            for dc in range(3):
                total = None
                if dc == 1:
                    total = nn_dot(hint_v[b, pl.ds(start, BLOCK), :], cw_v[...])
                for dr in range(3):
                    for h in halves:
                        lhs = act[h, b, pl.ds(start + dr * ROW, BLOCK), :]
                        part = nn_dot(lhs, w_v[3 * dr + dc, channels * h:channels * (h + 1), :])
                        total = part if total is None else total + part
                y[dc] = total
            for r in range(BLOCK // ROW):
                where = pl.ds(r * ROW, ROW)
                total = y[1, where, :] + shift(y[0, where, :], 1) + shift(y[2, where, :], -1)
                x = x_ext[b, pl.ds(start + (r + 1) * ROW, ROW), :].astype(F32)
                out_v[b, pl.ds(start + r * ROW, ROW), :] = (x + total).astype(BF16)
            return carry
        lax.fori_loop(0, samples * cells // BLOCK, step, 0)

    def transposed(halves):
        def step(i, carry):
            b = i // (cells // BLOCK)
            start = pl.multiple_of(lax.rem(i, cells // BLOCK) * BLOCK, BLOCK)
            for h in halves:
                for dc in range(3):
                    total = None
                    for dr in range(3):
                        lhs = g_ext[b, pl.ds(start + (2 - dr) * ROW, BLOCK), :]
                        part = nt_dot(lhs, w_v[3 * dr + dc, channels * h:channels * (h + 1), :])
                        total = part if total is None else total + part
                    y[dc] = total
                for r in range(BLOCK // ROW):
                    where = pl.ds(r * ROW, ROW)
                    total = y[1, where, :] + shift(y[0, where, :], -1) + shift(y[2, where, :], 1)
                    dact[h, b, pl.ds(start + r * ROW, ROW), :] = total
            return carry
        lax.fori_loop(0, samples * cells // BLOCK, step, 0)

    def shift_gradient():
        def step(i, carry):
            b = i // rows
            start = pl.multiple_of(lax.rem(i, rows) * ROW, ROW)
            g = g_ext[b, pl.ds(start + ROW, ROW), :].astype(F32)
            shifted[0, b, pl.ds(start, ROW), :] = shift(g, -1).astype(BF16)
            shifted[1, b, pl.ds(start, ROW), :] = shift(g, 1).astype(BF16)
            return carry
        lax.fori_loop(0, samples * rows, step, 0)

    def control_gradient(offset):
        total = sum(tn_dot(hint_v[b], g_ext[b, inner, :]) for b in range(samples))
        grads[offset:offset + channels, :] = total.astype(BF16)

    def kernel_gradient(halves, row):
        width = channels * len(halves)
        for h in halves:
            for dc in range(3):
                total = None
                for b in range(samples):
                    g = g_ext[b, inner, :] if dc == 1 else shifted[dc // 2, b]
                    lhs = act[h, b, row * ROW:row * ROW + cells, :]
                    part = tn_dot(lhs, g)
                    total = part if total is None else total + part
                base = (3 * row + dc) * width + h * channels
                grads[base:base + channels, :] = total.astype(BF16)

    def norm_backward(halves):
        lines = []
        for b in range(samples):
            middle = stat_v[0, b:b + 1, :]
            scale = stat_v[1, b:b + 1, :]

            def step(i, sums):
                where = pl.ds(pl.multiple_of(i * CHUNK, CHUNK), CHUNK)
                outer = pl.ds(pl.multiple_of(i * CHUNK + ROW, CHUNK), CHUNK)
                xhat = (x_ext[b, outer, :].astype(F32) - middle) * scale
                out = []
                for n, h in enumerate(halves):
                    u = xhat * gain_ref[h:h + 1, :] + bias_ref[h:h + 1, :]
                    s = sigmoid(u)
                    du = dact[h, b, where, :] * s * (1.0 + u * (1.0 - s))
                    dact[h, b, where, :] = du
                    out.append(sums[2 * n] + fold(du))
                    out.append(sums[2 * n + 1] + fold(du * xhat))
                return tuple(out)
            start = tuple(jnp.zeros((8, channels), F32) for _ in range(2 * len(halves)))
            sums = lax.fori_loop(0, cells // CHUNK, step, start)
            lines.append([s.sum(axis=0, keepdims=True) for s in sums])
        order = []
        for n in range(len(halves)):
            order += [lines[b][2 * n] for b in range(samples)]
            order += [lines[b][2 * n + 1] for b in range(samples)]
        for n in range(len(order), 8):
            order.append(jnp.zeros((1, channels), F32))
        return jnp.concatenate(order, axis=0)

    def part_geometry(p):
        return ORDERS[p], part_rows(size, p)

    stride = tuple(max(part_rows(size, p)[stage] for p in range(3)) for stage in range(3))

    def scatter_copies(p, stage):
        axes, ns = part_geometry(p)
        axis, n = axes[stage], ns[stage]
        src = (grads, s1, s2)[stage]
        dst = (r1, r2, r3)[stage]
        base = p * PART if stage == 0 else p * stride[stage - 1]
        copies = []
        for k in range(1, size[axis]):
            to = lax.rem(mine[axis] + k, size[axis])
            where = pl.ds(pl.multiple_of(base + to * n, 16), n)
            inbox = dst.at[p, pl.ds((k - 1) * n, n), :]
            copies.append(send(f"rs {p} {stage} {k}", src.at[where, :], inbox, peer(axis, k)))
        return copies

    def final_offset(p):
        axes, ns = part_geometry(p)
        return p * PART + sum(mine[a] * n for a, n in zip(axes, ns))

    def scatter_sum(p, stage):
        axes, ns = part_geometry(p)
        axis, n = axes[stage], ns[stage]
        src = (grads, s1, s2)[stage]
        inbox = (r1, r2, r3)[stage]
        base = p * PART if stage == 0 else p * stride[stage - 1]
        own = base + mine[axis] * n
        if stage == 0:
            dst, to = s1, p * stride[0]
        elif stage == 1:
            dst, to = s2, p * stride[1]
        else:
            dst, to = gathered, final_offset(p)
        chunk = 16

        def step(i, carry):
            total = src[pl.ds(pl.multiple_of(own + i * chunk, 16), chunk), :].astype(F32)
            for k in range(size[axis] - 1):
                total += inbox[p, pl.ds(pl.multiple_of(k * n + i * chunk, 16), chunk), :].astype(F32)
            dst[pl.ds(pl.multiple_of(to + i * chunk, 16), chunk), :] = total.astype(BF16)
            return carry
        lax.fori_loop(0, n // chunk, step, 0)

    def gather_copies(p, stage):
        axes, ns = part_geometry(p)
        axis, n = axes[stage], ns[stage]
        offset = p * PART + sum(mine[a] * m for a, m in zip(axes[:stage + 1], ns[:stage + 1]))
        where = pl.ds(pl.multiple_of(offset, 16), n)
        return [
            send(f"ag {p} {stage} {k}", gathered.at[where, :], gathered.at[where, :], peer(axis, k))
            for k in range(1, size[axis])
        ]

    def gather_wait(p, stage):
        axes, ns = part_geometry(p)
        axis, n = axes[stage], ns[stage]
        base = p * PART + sum(mine[a] * m for a, m in zip(axes[:stage], ns[:stage]))
        for k in range(1, size[axis]):
            source = lax.rem(mine[axis] + size[axis] - k, size[axis])
            where = pl.ds(pl.multiple_of(base + source * n, 16), n)
            send(f"ag {p} {stage} {k}", gathered.at[where, :], gathered.at[where, :], peer(axis, k)).wait()

    def start(copies):
        for c in copies:
            c.start()

    def wait(copies):
        for c in copies:
            c.wait()

    def reduce_rest(parts):
        for stage in range(3):
            for p in parts:
                wait(scatter_copies(p, stage))
                scatter_sum(p, stage)
                start(scatter_copies(p, stage + 1) if stage < 2 else gather_copies(p, 2))
        for stage in (2, 1, 0):
            for p in parts:
                gather_wait(p, stage)
                if stage > 0:
                    start(gather_copies(p, stage - 1))

    def finish(parts, halves, base):
        width = channels * len(halves)
        copies = []
        if len(halves) == 1:
            for tap in range(9):
                copies.append(local(f"out {tap}", gathered.at[pl.ds(tap * width, width), :], conv_out.at[tap, pl.ds(0, width), :]))
                copies.append(local(f"zero {tap}", zeros_v, conv_out.at[tap, pl.ds(width, channels), :]))
        else:
            for tap in range(9):
                copies.append(local(f"out {tap}", gathered.at[pl.ds(tap * width, width), :], conv_out.at[tap]))
        start(copies)

        ctrl_out[...] = gathered[base:base + channels, :].astype(F32)
        wait(copies)

    @pl.when(seg == 0)
    def _encoder():
        halves = (0,)
        load = loads(True)
        load["main"]().wait()
        halo = edges("lat", x_ext, (x_ext.at[:, first, :], x_ext.at[:, last, :]), 0)
        start(halo)
        local_stats(x_ext, ROW, "a x")
        copies = exchange("a x", "x")
        start(copies)
        wait(copies)
        mean, spread = merge(arrivals("a x", "x", True), float(cells))
        s_send[slots.buffer("a z"), 0:samples, :] = mean
        s_send[slots.buffer("a z"), samples:2 * samples, :] = spread
        copies = exchange("a z", "z")
        start(copies)
        wait(copies)
        mean, spread = merge(arrivals("a z", "z", True), float(cells * NX))
        finish_stats(mean, spread, channels // GROUPS)
        wait(halo)
        activate(halves)
        for key in ("hint", "weight", "control"):
            load[key]().wait()
        forward(halves)
        ahead = [send("o", out_v, x_ext.at[:, inner, :], at(space, 1))]
        ahead += edges("o", x_ext, (out_v.at[:, pl.ds(0, ROW), :], out_v.at[:, pl.ds(cells - ROW, ROW), :]), 1)
        save = local("acts", out_v, acts_hbm)
        start(ahead)
        save.start()
        local_stats(out_v, 0, "b x")
        copies = exchange("b x", "x")
        start(copies)
        wait(copies)
        mean, spread = merge(arrivals("b x", "x", True), float(cells))
        s_send[slots.buffer("b z"), 0:samples, :] = mean
        s_send[slots.buffer("b z"), samples:2 * samples, :] = spread
        stats = exchange("b z", "z", core=1)
        start(stats)
        for c in ahead + stats:
            c.wait_send()
        save.wait()
        back = [send("g", out_v, g_ext.at[:, inner, :], at(space, 0))]
        back += edges("g", g_ext, (out_v.at[:, pl.ds(0, ROW), :], out_v.at[:, pl.ds(cells - ROW, ROW), :]), 0)
        for c in back:
            c.wait_recv()
        zero_outside(g_ext)
        shift_gradient()
        for row in range(3):
            kernel_gradient(halves, row)
        control_gradient(kernel_rows)
        grads[kernel_rows + channels:2 * PART, :] = jnp.zeros((2 * PART - kernel_rows - channels, channels), BF16)
        for p in (0, 1):
            start(scatter_copies(p, 0))
        transposed(halves)
        sums = norm_backward(halves)
        sums = small_sum("e", ("x", "z", "y"), sums)
        blank = jnp.zeros((1, channels), F32)
        bias_out[0:1, :] = sums[0:samples].sum(axis=0, keepdims=True)
        gain_out[0:1, :] = sums[samples:2 * samples].sum(axis=0, keepdims=True)
        bias_out[1:2, :] = blank
        gain_out[1:2, :] = blank
        zeros_v[...] = jnp.zeros(zeros_v.shape, BF16)
        reduce_rest((0, 1))
        finish((0, 1), halves, kernel_rows)

    @pl.when(seg == 1)
    def _decoder():
        halves = (0, 1)
        load = loads(False)
        load["main"]().wait()
        halo = edges("cot", g_ext, (g_ext.at[:, first, :], g_ext.at[:, last, :]), 1)
        start(halo)
        load["hint"]().wait()
        control_gradient(2 * kernel_rows)
        grads[2 * kernel_rows + channels:3 * PART, :] = jnp.zeros((3 * PART - 2 * kernel_rows - channels, channels), BF16)
        shift_gradient()
        load["weight"]().wait()
        load["control"]().wait()
        wait(halo)
        zero_outside(g_ext)
        transposed(halves)
        ahead = [send("o", out_v, x_ext.at[:, inner, :], at(space, 1))]
        ahead += edges("o", x_ext, (out_v.at[:, pl.ds(0, ROW), :], out_v.at[:, pl.ds(cells - ROW, ROW), :]), 1)
        stats = exchange("b z", "z", core=1)
        for c in ahead + stats:
            c.wait_recv()
        mean, spread = merge(arrivals("b z", "z", False), float(cells * NX))
        finish_stats(mean, spread, 2 * channels // GROUPS)
        sums = norm_backward(halves)
        sums = small_sum("c", ("x", "z"), sums)
        total = float(cells * space_count)
        width = 2 * channels // GROUPS
        for h in halves:
            gain = gain_ref[h:h + 1, :]
            stat_v[2 + h] = group_mean(sums * gain, width) / total
        for b in range(samples):
            middle = stat_v[0, b:b + 1, :]
            scale = stat_v[1, b:b + 1, :]

            def step(i, carry):
                where = pl.ds(pl.multiple_of(i * CHUNK, CHUNK), CHUNK)
                outer = pl.ds(pl.multiple_of(i * CHUNK + ROW, CHUNK), CHUNK)
                xhat = (x_ext[b, outer, :].astype(F32) - middle) * scale
                dj = []
                for h in halves:
                    m1 = stat_v[2 + h, 4 * h + b:4 * h + b + 1, :]
                    m2 = stat_v[2 + h, 4 * h + 2 + b:4 * h + 3 + b, :]
                    dx = dact[h, b, where, :] * gain_ref[h:h + 1, :]
                    dj.append((dx - m1 - xhat * m2) * scale)
                dh = (g_ext[b, outer, :].astype(F32) + dj[0]).astype(BF16)
                dskip = dj[1].astype(BF16)
                out_v[b, where, :] = (dh.astype(F32) + dskip.astype(F32)).astype(BF16)
                return carry
            lax.fori_loop(0, cells // CHUNK, step, 0)
        back = [send("g", out_v, g_ext.at[:, inner, :], at(space, 0))]
        back += edges("g", g_ext, (out_v.at[:, pl.ds(0, ROW), :], out_v.at[:, pl.ds(cells - ROW, ROW), :]), 0)
        start(back)
        activate(halves)
        for row in range(3):
            kernel_gradient(halves, row)
        for p in (0, 1, 2):
            start(scatter_copies(p, 0))
        for c in back:
            c.wait_send()
        forward(halves)
        save = local("acts", out_v, acts_hbm)
        save.start()
        sums = small_sum("f", ("y",), sums)
        for h in halves:
            bias_out[h:h + 1, :] = sums[4 * h:4 * h + 2].sum(axis=0, keepdims=True)
            gain_out[h:h + 1, :] = sums[4 * h + 2:4 * h + 4].sum(axis=0, keepdims=True)
        reduce_rest((0, 1, 2))
        finish((0, 1, 2), halves, 2 * kernel_rows)
        save.wait()


ORDERS = (("x", "y", "z"), ("y", "x", "z"), ("z", "x", "y"))


def part_rows(size, p):
    rows, out = PART, []
    for axis in ORDERS[p]:
        rows //= size[axis]
        out.append(rows)
    return tuple(out)


class Names(Slots):
    def __init__(self):
        super().__init__()
        self.buffers = Slots()
        self.inboxes = Slots()

    def buffer(self, name):
        return self.buffers(name)

    def inbox(self, name):
        return self.inboxes(name)


def on_device(grid, latents, hint, cotangent, conv_weight, ctrl_weight, norm_gain, norm_bias):
    NZ, NX, NY = grid
    samples, frames, rows, cols, channels = latents.shape
    cells = rows * cols
    ext = cells + 2 * ROW
    dims = (NZ, NX, NY, samples, rows, channels)
    flat = lambda a: a.reshape(samples, cells, channels)
    vmem = pl.BlockSpec(memory_space=pltpu.VMEM)
    anywhere = pl.BlockSpec(memory_space=pl.ANY)
    size = {"x": NX, "y": NY, "z": NZ}
    stride = [max(part_rows(size, p)[stage] for p in range(3)) for stage in range(3)]
    inbox = [max(part_rows(size, p)[stage] * (size[ORDERS[p][stage]] - 1) for p in range(3)) for stage in range(3)]
    out = pl.pallas_call(
        functools.partial(body, dims, Names()),
        out_shape=(
            jax.ShapeDtypeStruct((samples, cells, channels), BF16),
            jax.ShapeDtypeStruct((9, 2 * channels, channels), BF16),
            jax.ShapeDtypeStruct((channels, channels), F32),
            jax.ShapeDtypeStruct((2, channels), F32),
            jax.ShapeDtypeStruct((2, channels), F32),
        ),
        in_specs=[anywhere] * 5 + [vmem] * 2,
        out_specs=(anywhere, anywhere, vmem, vmem, vmem),
        scratch_shapes=[
            pltpu.VMEM((samples, ext, channels), BF16),
            pltpu.VMEM((samples, ext, channels), BF16),
            pltpu.VMEM((samples, cells, channels), BF16),
            pltpu.VMEM((9, 2 * channels, channels), BF16),
            pltpu.VMEM((channels, channels), BF16),
            pltpu.VMEM((2, samples, ext, channels), BF16),
            pltpu.VMEM((3, 2 * ROW, channels), F32),
            pltpu.VMEM((2, samples, cells, channels), F32),
            pltpu.VMEM((2, samples, cells, channels), BF16),
            pltpu.VMEM((samples, cells, channels), BF16),
            pltpu.VMEM((12, 8, channels), F32),
            pltpu.VMEM((64, 8, channels), F32),
            pltpu.VMEM((4, 8, channels), F32),
            pltpu.VMEM((3 * PART, channels), BF16),
            pltpu.VMEM((3, inbox[0], channels), BF16),
            pltpu.VMEM((3, inbox[1], channels), BF16),
            pltpu.VMEM((3, inbox[2], channels), BF16),
            pltpu.VMEM((3 * stride[0], channels), BF16),
            pltpu.VMEM((3 * stride[1], channels), BF16),
            pltpu.VMEM((3 * PART, channels), BF16),
            pltpu.VMEM((channels, channels), BF16),
            pltpu.VMEM((channels, channels), F32),
            pltpu.SemaphoreType.DMA((160,)),
            pltpu.SemaphoreType.DMA((160,)),
            pltpu.SemaphoreType.DMA((200,)),
        ],
        compiler_params=pltpu.CompilerParams(
            collective_id=0, has_side_effects=True, vmem_limit_bytes=60 * 1024 * 1024
        ),
    )(
        flat(latents), flat(hint), flat(cotangent), conv_weight[0], ctrl_weight[0],
        norm_gain.reshape(2, channels), norm_bias.reshape(2, channels),
    )
    acts, conv, ctrl, gain, bias = out
    return (
        acts.reshape((1,) + latents.shape),
        conv[None],
        ctrl[None],
        gain.reshape(1, 2 * channels),
        bias.reshape(1, 2 * channels),
    )


def grid_of(mesh):
    space = mesh.shape["space"]
    columns = 4 if space >= 32 else 2
    return (space // columns, columns, mesh.shape["dp"])


def solution(mesh):
    return jax.shard_map(
        functools.partial(on_device, grid_of(mesh)),
        mesh=mesh,
        in_specs=(
            P("dp", None, "space", None, None),
            P("dp", None, "space", None, None),
            P("dp", None, "space", None, None),
            P("segment", None, None, None),
            P("segment", None, None),
            P("segment", None),
            P("segment", None),
        ),
        out_specs=(
            P("segment", "dp", None, "space", None, None),
            P("segment", None, None, None),
            P("segment", None, None),
            P("segment", None),
            P("segment", None),
        ),
        check_vma=False,
    )
```

```python
import functools

import jax
import jax.numpy as jnp
from jax import lax
from jax.experimental import pallas as pl
from jax.experimental.pallas import tpu as pltpu
from jax.sharding import PartitionSpec as P

MESH = pl.DeviceIdType.MESH
F32 = jnp.float32
BF16 = jnp.bfloat16
EPS = 1e-05
GROUPS = 32
LANES = 128
UNIT = 2048
CHUNK = 32
HIGH = lax.Precision.HIGHEST

ORDERS = (("x", "y", "z"), ("y", "x", "z"), ("z", "x", "y"))
PARTS = {1: ((0, 2 * UNIT), (1, 2 * UNIT), (2, UNIT)), 2: ((0, 3 * UNIT), (1, 3 * UNIT), (2, 2 * UNIT))}


def nt_dot(a, b, precision=None):
    return lax.dot_general(
        a, b, (((1,), (1,)), ((), ())), precision=precision, preferred_element_type=F32
    )


def tn_dot(a, b, precision=None):
    return lax.dot_general(
        a, b, (((0,), (0,)), ((), ())), precision=precision, preferred_element_type=F32
    )


def nn_dot(a, b):
    return jnp.dot(a, b, preferred_element_type=F32)


def sigmoid(v):
    return 1.0 / (1.0 + jnp.exp(-v))


def part_rows(size, halves, p):
    rows, out = PARTS[halves][p][1], []
    for axis in ORDERS[PARTS[halves][p][0]]:
        rows //= size[axis]
        out.append(rows)
    return tuple(out)


def largest(size, value):
    return [
        max(value(part_rows(size, halves, p), ORDERS[PARTS[halves][p][0]], stage) for halves in (1, 2) for p in range(3))
        for stage in range(3)
    ]


class Slots:
    def __init__(self):
        self.index = {}

    def __call__(self, name):
        return self.index.setdefault(name, len(self.index))


class Names(Slots):
    def __init__(self):
        super().__init__()
        self.local = Slots()
        self.boxes = {}

    def box(self, name, count):
        return self.boxes.setdefault(name, (sum(n for _, n in self.boxes.values()), count))[0]


def body(
    dims,
    slots,
    lat_hbm, hint_hbm, cot_hbm, w_hbm, cw_hbm, gain_ref, bias_ref,
    acts_hbm, grads_hbm, gain_out, bias_out,
    x_ext, g_ext, hint_v, w_v, cw_v, wb, act, act_t, g3, y, dact, out_v, last_v,
    columns, sums_v, gain_c, bias_c,
    s_recv, grads, r1, r2, r3, s1, s2, gathered,
    send_sem, recv_sem, local_sem,
):
    NZ, NX, NY, samples, rows, channels = dims
    cells = rows * LANES
    wide = samples * LANES
    space_count = NZ * NX
    seg = lax.axis_index("segment")
    space = lax.axis_index("space")
    dp = lax.axis_index("dp")
    zi = space // NX
    xi = lax.rem(space, NX)
    other = 1 - seg
    up = lax.rem(space + space_count - 1, space_count)
    down = lax.rem(space + 1, space_count)
    size = {"x": NX, "y": NY, "z": NZ}
    mine = {"x": xi, "y": dp, "z": zi}

    def peer(axis, k, core=None):
        if axis == "x":
            place = {"space": zi * NX + lax.rem(xi + k, NX), "dp": dp}
        elif axis == "z":
            place = {"space": lax.rem(zi + k, NZ) * NX + xi, "dp": dp}
        else:
            place = {"space": space, "dp": lax.rem(dp + k, NY)}
        place["segment"] = seg if core is None else core
        return place

    def at(space_id, core):
        return {"space": space_id, "dp": dp, "segment": core}

    def send(name, src, dst, place):
        slot = slots(name)
        return pltpu.make_async_remote_copy(
            src_ref=src, dst_ref=dst, send_sem=send_sem.at[slot], recv_sem=recv_sem.at[slot],
            device_id=(place["segment"], place["space"], place["dp"]), device_id_type=MESH,
        )

    def local(name, src, dst):
        return pltpu.make_async_copy(src, dst, local_sem.at[slots.local(name)])

    def start(copies):
        for c in copies:
            c.start()

    def wait(copies):
        for c in copies:
            c.wait()

    inner = pl.ds(1, rows)

    def sample(b):
        return pl.ds(b * LANES, LANES)

    def loads(is_encoder, key):
        if key == "weight":
            return [local(key, w_hbm, w_v)]
        if key == "control":
            return [local(key, cw_hbm, cw_v)]
        if key == "hint":
            return [local(f"{key} {b}", hint_hbm.at[b], hint_v.at[:, :, sample(b)]) for b in range(samples)]
        source, target = (lat_hbm, x_ext) if is_encoder else (cot_hbm, g_ext)
        return [local(f"{key} {b}", source.at[b], target.at[inner, :, sample(b)]) for b in range(samples)]

    @pl.when(seg == 0)
    def _():
        for key in ("main", "weight", "control", "hint"):
            start(loads(True, key))

    @pl.when(seg == 1)
    def _():
        for key in ("main", "weight", "hint", "control"):
            start(loads(False, key))

    barrier = pltpu.get_barrier_semaphore()
    places = [peer("x", k) for k in range(1, NX)]
    places += [peer("y", k) for k in range(1, NY)]
    places += [peer("z", k) for k in range(1, NZ)]
    places += [peer("z", k, other) for k in range(NZ)]
    places += [at(n, c) for n in (up, down) for c in (seg, other)]
    for place in places:
        pl.semaphore_signal(
            barrier, inc=1,
            device_id=(place["segment"], place["space"], place["dp"]), device_id_type=MESH,
        )

    line = lax.broadcasted_iota(jnp.int32, (8, LANES), 0)
    ones = jnp.ones((8, LANES), F32)
    first_lane = jnp.where(lax.broadcasted_iota(jnp.int32, (8, LANES), 1) == 0, 1.0, 0.0)

    def to_row(block, pick=None):
        return nt_dot(ones if pick is None else pick, block, HIGH)[0:1, :]

    def to_column(value, k):
        return tn_dot(value, jnp.where(line == k, 1.0, 0.0), HIGH)

    def eight(parts):
        count = sum(p.shape[0] for p in parts)
        if count < 8:
            parts = parts + [jnp.zeros((8 - count, parts[0].shape[1]), F32)]
        return jnp.concatenate(parts, axis=0)

    gain_c[...] = to_column(eight([gain_ref[...]]), 0)
    bias_c[...] = to_column(eight([bias_ref[...]]), 0)

    lane = lax.broadcasted_iota(jnp.int32, (channels, channels), 0).astype(F32)
    lane_t = lax.broadcasted_iota(jnp.int32, (channels, channels), 1).astype(F32)

    def group_mean(values, width):
        same = jnp.floor((lane + 0.5) / width) == jnp.floor((lane_t + 0.5) / width)
        return jnp.dot(
            values, jnp.where(same, 1.0, 0.0), precision=HIGH, preferred_element_type=F32
        ) / width

    def edges(name, ref, src, core):
        return [
            send(name + " down", src[1], ref.at[0], at(down, core)),
            send(name + " up", src[0], ref.at[rows + 1], at(up, core)),
        ]

    def zero_outside(ref):
        blank = jnp.zeros(ref.shape[1:], ref.dtype)

        @pl.when(space == 0)
        def _():
            ref[0] = blank

        @pl.when(space == space_count - 1)
        def _():
            ref[rows + 1] = blank

    def chunks(step, width=CHUNK):
        def run(i, carry):
            step(pl.multiple_of(i * width, width))
            return carry
        lax.fori_loop(0, channels // width, run, 0)

    def local_stats(ref, base, name):
        def step(at_row):
            where = pl.ds(at_row, CHUNK)
            for b in range(samples):
                v = [ref[base + r, where, sample(b)].astype(F32) for r in range(rows)]
                mean = jnp.sum(sum(v), axis=1, keepdims=True) / cells
                sums_v[b, where, :] = jnp.broadcast_to(mean, (CHUNK, LANES))
                sums_v[samples + b, where, :] = sum(jnp.square(t - mean) for t in v)
        chunks(step)
        lines = [to_row(sums_v[b], first_lane) for b in range(samples)]
        lines += [to_row(sums_v[samples + b]) for b in range(samples)]
        put(name, "x", eight(lines))

    def put(name, axis, value):
        s_recv[slots.box(name, size[axis]) + mine[axis]] = value

    def exchange(name, axis, core=None, landing=False):
        base = slots.box(name, size[axis])
        copies = []
        for k in range(0 if core is not None else 1, size[axis]):
            owner = lax.rem(mine[axis] + size[axis] - k, size[axis]) if landing else mine[axis]
            copies.append(send(f"{name} {k}", s_recv.at[base + mine[axis]], s_recv.at[base + owner], peer(axis, k, core)))
        return copies

    def arrivals(name, axis):
        base = slots.box(name, size[axis])
        return [s_recv.at[base + k] for k in range(size[axis])]

    def small_wait(name, axis):
        wait(exchange(name, axis, landing=True))

    def merge(refs, count):
        mean = sum(r[0:samples, :] for r in refs) / len(refs)
        spread = sum(r[samples:2 * samples, :] for r in refs)
        apart = sum(jnp.square(r[0:samples, :] - mean) for r in refs)
        return mean, spread + count * apart

    def finish_stats(mean, spread, width):
        total = cells * space_count
        padded = eight([mean])
        middle = group_mean(padded, width)
        offset = padded - middle
        var = group_mean(eight([spread]) / total + offset * offset, width)
        scale = lax.rsqrt(var + EPS)
        for b in range(samples):
            columns[b] = to_column(middle, b)
            columns[samples + b] = to_column(scale, b)

    def activate(halves):
        for h in halves:
            def step(at_row):
                where = pl.ds(at_row, CHUNK)
                inside = pl.ds(pl.multiple_of(at_row + h * channels, CHUNK), CHUNK)
                gain, bias = gain_c[inside, :], bias_c[inside, :]
                for b in range(samples):
                    middle, rate = columns[b, where, :], columns[samples + b, where, :]
                    for r in range(rows + 2):
                        xhat = (x_ext[r, where, sample(b)].astype(F32) - middle) * rate
                        u = xhat * gain + bias
                        a = (u * sigmoid(u)).astype(BF16)
                        act[r, inside, sample(b)] = a
                        act_t[inside, pl.ds(r * wide + b * LANES, LANES)] = a
            chunks(step)
        blank = jnp.zeros((2 * channels, wide), BF16)
        for r, edge in ((0, 0), (rows + 1, space_count - 1)):
            @pl.when(space == edge)
            def _():
                act[r] = blank
                act_t[:, r * wide:(r + 1) * wide] = blank

    lanes = lax.broadcasted_iota(jnp.int32, (channels, LANES), 1)

    def shift(v, step):
        column = 0 if step == 1 else LANES - 1
        return jnp.where(lanes[:v.shape[0]] != column, pltpu.roll(v, step % LANES, axis=1), 0.0)

    def forward(halves, target):
        width = channels * len(halves)

        def step(r, carry):
            total = None
            for dr in range(3):
                part = nn_dot(w_v[dr, :, 0:width], act[r + dr, 0:width, :])
                total = part if total is None else total + part
            y[0:3 * channels, :] = total
            y[3 * channels:4 * channels, :] = tn_dot(cw_v[...], hint_v[r])
            for b in range(samples):
                def tap(dc):
                    return y[dc * channels:(dc + 1) * channels, sample(b)]
                total = tap(1) + tap(3) + shift(tap(0), 1) + shift(tap(2), -1)
                x = x_ext[r + 1, :, sample(b)].astype(F32)
                target[r, :, sample(b)] = (x + total).astype(BF16)
            return carry
        lax.fori_loop(0, rows, step, 0)

    def turn_weights(halves):
        count = -(-channels * len(halves) // LANES)
        for dc in range(3):
            def block(j, carry):
                where = pl.ds(pl.multiple_of(j * LANES, LANES), LANES)
                taps = [w_v[2 - d, dc * channels:(dc + 1) * channels, where] for d in range(3)]
                wb[dc, where, :] = jnp.concatenate(taps, axis=0).T
                return carry
            lax.fori_loop(0, count, block, 0)

    def transposed(halves):
        def step(r, carry):
            g = g_ext[pl.ds(r, 3)].reshape(3 * channels, wide)
            for h in halves:
                for dc in range(3):
                    y[dc * channels:(dc + 1) * channels, :] = nn_dot(wb[dc, h * channels:(h + 1) * channels, :], g)
                for b in range(samples):
                    def tap(dc):
                        return y[dc * channels:(dc + 1) * channels, sample(b)]
                    dact[h, r, :, sample(b)] = tap(1) + shift(tap(0), -1) + shift(tap(2), 1)
            return carry
        lax.fori_loop(0, rows, step, 0)

    def shift_gradient():
        def step(r, carry):
            for b in range(samples):
                g = g_ext[r + 1, :, sample(b)]
                where = pl.ds(pl.multiple_of(r * wide + b * LANES, LANES), LANES)
                v = g.astype(F32)
                g3[0:channels, where] = shift(v, -1).astype(BF16)
                g3[channels:2 * channels, where] = g
                g3[2 * channels:3 * channels, where] = shift(v, 1).astype(BF16)
            return carry
        lax.fori_loop(0, rows, step, 0)

    def blocks(value, base):
        count = value.shape[0]
        for j in range(value.shape[1] // LANES):
            grads[base + j * count:base + (j + 1) * count, :] = value[:, j * LANES:(j + 1) * LANES].astype(BF16)

    def control_gradient(base):
        total = None
        for r in range(rows):
            where = pl.ds(r * wide, wide)
            part = nt_dot(hint_v[r], g3[channels:2 * channels, where])
            total = part if total is None else total + part
        blocks(jnp.concatenate([total, jnp.zeros((channels, 3 * LANES - channels), F32)], axis=1), base)

    def kernel_gradient(halves, dr):
        width = 3 * LANES if len(halves) == 1 else 2 * channels
        total = nt_dot(g3[...], act_t[0:width, dr * wide:(dr + rows) * wide])
        blocks(total, dr * 3 * channels * (width // LANES))

    def norm_backward(halves):
        for h in halves:
            def step(at_row):
                where = pl.ds(at_row, CHUNK)
                inside = pl.ds(pl.multiple_of(at_row + h * channels, CHUNK), CHUNK)
                gain, bias = gain_c[inside, :], bias_c[inside, :]
                for b in range(samples):
                    middle, rate = columns[b, where, :], columns[samples + b, where, :]
                    first = second = None
                    for r in range(rows):
                        xhat = (x_ext[r + 1, where, sample(b)].astype(F32) - middle) * rate
                        u = xhat * gain + bias
                        s = sigmoid(u)
                        du = dact[h, r, where, sample(b)] * s * (1.0 + u * (1.0 - s))
                        dact[h, r, where, sample(b)] = du
                        first = du if first is None else first + du
                        second = du * xhat if second is None else second + du * xhat
                    sums_v[4 * h + b, where, :] = first
                    sums_v[4 * h + samples + b, where, :] = second
            chunks(step)
        return eight([to_row(sums_v[k]) for k in range(4 * len(halves))])

    stride = tuple(largest(size, lambda ns, axes, stage: ns[stage]))

    def part_geometry(p, halves):
        parts = PARTS[halves]
        base = sum(n for _, n in parts[:p])
        return ORDERS[parts[p][0]], part_rows(size, halves, p), base

    def stage_base(p, halves, stage):
        base = part_geometry(p, halves)[2]
        return base if stage == 0 else p * stride[stage - 1]

    def scatter_copies(p, halves, stage):
        axes, ns, _ = part_geometry(p, halves)
        axis, n = axes[stage], ns[stage]
        src = (grads, s1, s2)[stage]
        dst = (r1, r2, r3)[stage]
        base = stage_base(p, halves, stage)
        copies = []
        for k in range(1, size[axis]):
            to = lax.rem(mine[axis] + k, size[axis])
            where = pl.ds(pl.multiple_of(base + to * n, 16), n)
            inbox = dst.at[p, pl.ds((k - 1) * n, n), :]
            copies.append(send(f"rs {p} {stage} {k}", src.at[where, :], inbox, peer(axis, k)))
        return copies

    def scatter_sum(p, halves, stage):
        axes, ns, part_base = part_geometry(p, halves)
        axis, n = axes[stage], ns[stage]
        src = (grads, s1, s2)[stage]
        inbox = (r1, r2, r3)[stage]
        own = stage_base(p, halves, stage) + mine[axis] * n
        if stage == 0:
            dst, to = s1, p * stride[0]
        elif stage == 1:
            dst, to = s2, p * stride[1]
        else:
            dst, to = gathered, part_base + sum(mine[a] * m for a, m in zip(axes, ns))
        chunk = 64 if n % 64 == 0 else 16

        def step(i, carry):
            total = src[pl.ds(pl.multiple_of(own + i * chunk, 16), chunk), :].astype(F32)
            for k in range(size[axis] - 1):
                total += inbox[p, pl.ds(pl.multiple_of(k * n + i * chunk, 16), chunk), :].astype(F32)
            dst[pl.ds(pl.multiple_of(to + i * chunk, 16), chunk), :] = total.astype(BF16)
            return carry
        lax.fori_loop(0, n // chunk, step, 0)

    def gather_copies(p, halves, stage):
        axes, ns, part_base = part_geometry(p, halves)
        axis, n = axes[stage], ns[stage]
        offset = part_base + sum(mine[a] * m for a, m in zip(axes[:stage + 1], ns[:stage + 1]))
        where = pl.ds(pl.multiple_of(offset, 16), n)
        return [
            send(f"ag {p} {stage} {k}", gathered.at[where, :], gathered.at[where, :], peer(axis, k))
            for k in range(1, size[axis])
        ]

    def gather_wait(p, halves, stage):
        axes, ns, part_base = part_geometry(p, halves)
        axis, n = axes[stage], ns[stage]
        base = part_base + sum(mine[a] * m for a, m in zip(axes[:stage], ns[:stage]))
        for k in range(1, size[axis]):
            source = lax.rem(mine[axis] + size[axis] - k, size[axis])
            where = pl.ds(pl.multiple_of(base + source * n, 16), n)
            send(f"ag {p} {stage} {k}", gathered.at[where, :], gathered.at[where, :], peer(axis, k)).wait()

    def reduce_rest(halves, name, axes, value):
        def small_start(stage):
            put(f"{name} {stage}", axes[stage], value)
            start(exchange(f"{name} {stage}", axes[stage]))

        small_start(0)
        for stage in range(3):
            for p in range(3):
                wait(scatter_copies(p, halves, stage))
                scatter_sum(p, halves, stage)
                start(scatter_copies(p, halves, stage + 1) if stage < 2 else gather_copies(p, halves, 2))
            if stage < len(axes):
                small_wait(f"{name} {stage}", axes[stage])
                value = sum(r[...] for r in arrivals(f"{name} {stage}", axes[stage]))
                if stage + 1 < len(axes):
                    small_start(stage + 1)
        for stage in (2, 1, 0):
            for p in range(3):
                gather_wait(p, halves, stage)
                if stage > 0:
                    start(gather_copies(p, halves, stage - 1))
                else:
                    start([part_out(p, halves)])
        return value

    def part_out(p, halves):
        base, n = part_geometry(p, halves)[2], PARTS[halves][p][1]
        return local(f"part {p}", gathered.at[pl.ds(base, n), :], grads_hbm.at[pl.ds(base, n), :])

    def saves(source):
        return [local(f"acts {b}", source.at[:, :, sample(b)], acts_hbm.at[b]) for b in range(samples)]

    def clear_tail(halves):
        used = 3 * 3 * channels * (3 if halves == 1 else 5) + 3 * channels
        total = sum(n for _, n in PARTS[halves])
        grads[used:total, :] = jnp.zeros((total - used, LANES), BF16)

    @pl.when(seg == 0)
    def _():
        wait(loads(True, "main"))
        local_stats(x_ext, 1, "a x")

    @pl.when(seg == 1)
    def _():
        wait(loads(False, "main"))
        clear_tail(2)
        shift_gradient()

    pl.semaphore_wait(barrier, len(places))

    @pl.when(seg == 0)
    def _encoder():
        halves = (0,)
        start(exchange("a x", "x"))
        halo = edges("lat", x_ext, (x_ext.at[1], x_ext.at[rows]), 0)
        start(halo)
        act_t[channels:3 * LANES, :] = jnp.zeros((3 * LANES - channels, act_t.shape[1]), BF16)
        clear_tail(1)
        small_wait("a x", "x")
        mean, spread = merge(arrivals("a x", "x"), float(cells))
        put("a z", "z", eight([mean, spread]))
        start(exchange("a z", "z"))
        wait(loads(True, "weight"))
        turn_weights(halves)
        small_wait("a z", "z")
        mean, spread = merge(arrivals("a z", "z"), float(cells * NX))
        finish_stats(mean, spread, channels // GROUPS)
        wait(halo)
        activate(halves)
        wait(loads(True, "hint"))
        wait(loads(True, "control"))
        forward(halves, out_v)
        ahead = [send("o", out_v, x_ext.at[inner], at(space, 1))]
        start(ahead)
        start(saves(out_v))
        local_stats(out_v, 0, "b x")
        start(exchange("b x", "x"))
        small_wait("b x", "x")
        mean, spread = merge(arrivals("b x", "x"), float(cells))
        put("b z", "z", eight([mean, spread]))
        stats = exchange("b z", "z", core=1)
        start(stats)
        halo = edges("o", x_ext, (out_v.at[0], out_v.at[rows - 1]), 1)
        start(halo)
        ahead += halo
        for c in ahead + stats:
            c.wait_send()
        wait(saves(out_v))
        send("g", out_v, g_ext.at[inner], at(space, 0)).wait_recv()
        shift_gradient()
        kernel_gradient(halves, 0)
        kernel_gradient(halves, 1)
        start(scatter_copies(0, 1, 0))
        kernel_gradient(halves, 2)
        start(scatter_copies(1, 1, 0))
        control_gradient(3 * 3 * channels * 3)
        start(scatter_copies(2, 1, 0))
        for c in edges("g", g_ext, (out_v.at[0], out_v.at[rows - 1]), 0):
            c.wait_recv()
        zero_outside(g_ext)
        transposed(halves)
        sums = norm_backward(halves)
        sums = reduce_rest(1, "e", ("x", "z", "y"), sums)
        blank = jnp.zeros((1, channels), F32)
        bias_out[...] = jnp.concatenate([sums[0:1] + sums[1:2], blank], axis=1)
        gain_out[...] = jnp.concatenate([sums[2:3] + sums[3:4], blank], axis=1)
        wait([part_out(p, len(halves)) for p in range(3)])

    @pl.when(seg == 1)
    def _decoder():
        halves = (0, 1)
        halo = edges("cot", g_ext, (g_ext.at[1], g_ext.at[rows]), 1)
        start(halo)
        wait(loads(False, "weight"))
        turn_weights(halves)
        wait(halo)
        zero_outside(g_ext)
        transposed(halves)
        wait(loads(False, "hint"))
        control_gradient(3 * 3 * channels * 5)
        wait(loads(False, "control"))
        send("o", out_v, x_ext.at[inner], at(space, 1)).wait_recv()
        for c in exchange("b z", "z", core=1, landing=True):
            c.wait_recv()
        mean, spread = merge(arrivals("b z", "z"), float(cells * NX))
        width = 2 * channels // GROUPS
        finish_stats(mean, spread, width)
        sums = norm_backward(halves)
        put("c x", "x", sums)
        start(exchange("c x", "x"))
        for c in edges("o", x_ext, (out_v.at[0], out_v.at[rows - 1]), 1):
            c.wait_recv()
        activate(halves)
        small_wait("c x", "x")
        sums = sum(r[...] for r in arrivals("c x", "x"))
        put("c z", "z", sums)
        start(exchange("c z", "z"))
        for dr in range(3):
            kernel_gradient(halves, dr)
        start(scatter_copies(1, 2, 0))
        small_wait("c z", "z")
        start(scatter_copies(2, 2, 0))
        sums = sum(r[...] for r in arrivals("c z", "z"))
        total = float(cells * space_count)
        for h in halves:
            gain = gain_ref[:, h * channels:(h + 1) * channels]
            means = group_mean(sums * gain, width) / total
            for k in range(4):
                columns[4 + 4 * h + k] = to_column(means, 4 * h + k)

        def step(at_row):
            where = pl.ds(at_row, CHUNK)
            gains = [gain_c[pl.ds(pl.multiple_of(at_row + h * channels, CHUNK), CHUNK), :] for h in halves]
            for b in range(samples):
                middle, rate = columns[b, where, :], columns[samples + b, where, :]
                means = [(columns[4 + 4 * h + b, where, :], columns[6 + 4 * h + b, where, :]) for h in halves]
                for r in range(rows):
                    xhat = (x_ext[r + 1, where, sample(b)].astype(F32) - middle) * rate
                    dj = []
                    for h in halves:
                        dx = dact[h, r, where, sample(b)] * gains[h]
                        dj.append((dx - means[h][0] - xhat * means[h][1]) * rate)
                    dh = (g_ext[r + 1, where, sample(b)].astype(F32) + dj[0]).astype(BF16)
                    dskip = dj[1].astype(BF16)
                    out_v[r, where, sample(b)] = (dh.astype(F32) + dskip.astype(F32)).astype(BF16)
        chunks(step)
        back = [send("g", out_v, g_ext.at[inner], at(space, 0))]
        back += edges("g", g_ext, (out_v.at[0], out_v.at[rows - 1]), 0)
        start(back)
        start(scatter_copies(0, 2, 0))
        forward(halves, last_v)
        start(saves(last_v))
        sums = reduce_rest(2, "f", ("y",), sums)
        bias_out[...] = jnp.concatenate([sums[0:1] + sums[1:2], sums[4:5] + sums[5:6]], axis=1)
        gain_out[...] = jnp.concatenate([sums[2:3] + sums[3:4], sums[6:7] + sums[7:8]], axis=1)
        wait([part_out(p, len(halves)) for p in range(3)])
        wait(saves(last_v))
        for c in back:
            c.wait_send()


def deliver(
    channels, acts_in, grads_in, gain_in, bias_in,
    acts_out, conv_out, ctrl_out, gain_out, bias_out, zeros_v, sem,
):
    seg = lax.axis_index("segment")
    high = 3 * channels

    def copies(count):
        out = [
            pltpu.make_async_copy(acts_in, acts_out, sem.at[0]),
        ]
        for dr in range(3):
            for j in range(5):
                target = conv_out.at[pl.ds(dr * high, high), pl.ds(j * LANES, LANES)]
                source = grads_in.at[pl.ds((dr * count + j) * high, high), :] if j < count else zeros_v
                out.append(pltpu.make_async_copy(source, target, sem.at[1 + 5 * dr + j]))
        return out

    def run(count):
        moves = copies(count)
        for c in moves:
            c.start()
        gain_out[...] = gain_in[...]
        bias_out[...] = bias_in[...]
        base, last = 3 * count * high, channels - 2 * LANES
        ctrl_out[:, 0:LANES] = grads_in[base:base + channels, :].astype(F32)
        ctrl_out[:, LANES:2 * LANES] = grads_in[base + channels:base + 2 * channels, :].astype(F32)
        ctrl_out[:, 2 * LANES:channels] = grads_in[base + 2 * channels:base + high, 0:last].astype(F32)
        for c in moves:
            c.wait()

    @pl.when(seg == 0)
    def _():
        zeros_v[...] = jnp.zeros(zeros_v.shape, BF16)
        run(3)

    @pl.when(seg == 1)
    def _():
        run(5)


def on_device(grid, latents, hint, cotangent, conv_weight, ctrl_weight, norm_gain, norm_bias):
    NZ, NX, NY = grid
    samples, frames, rows, cols, channels = latents.shape
    cells = rows * cols
    wide = samples * cols
    dims = (NZ, NX, NY, samples, rows, channels)
    turned = lambda a: a.transpose(0, 1, 2, 4, 3).reshape(samples, rows, channels, cols)
    vmem = pl.BlockSpec(memory_space=pltpu.VMEM)
    anywhere = pl.BlockSpec(memory_space=pl.ANY)
    size = {"x": NX, "y": NY, "z": NZ}
    stride = largest(size, lambda ns, axes, stage: ns[stage])
    inbox = largest(size, lambda ns, axes, stage: ns[stage] * (size[axes[stage]] - 1))
    total = max(sum(n for _, n in parts) for parts in PARTS.values())
    out = pl.pallas_call(
        functools.partial(body, dims, Names()),
        out_shape=(
            jax.ShapeDtypeStruct((samples, rows, channels, cols), BF16),
            jax.ShapeDtypeStruct((total, LANES), BF16),
            jax.ShapeDtypeStruct((1, 2 * channels), F32),
            jax.ShapeDtypeStruct((1, 2 * channels), F32),
        ),
        in_specs=[anywhere] * 5 + [vmem] * 2,
        out_specs=(anywhere, anywhere, vmem, vmem),
        scratch_shapes=[
            pltpu.VMEM((rows + 2, channels, wide), BF16),
            pltpu.VMEM((rows + 2, channels, wide), BF16),
            pltpu.VMEM((rows, channels, wide), BF16),
            pltpu.VMEM((3, 3 * channels, 2 * channels), BF16),
            pltpu.VMEM((channels, channels), BF16),
            pltpu.VMEM((3, 2 * channels, 3 * channels), BF16),
            pltpu.VMEM((rows + 2, 2 * channels, wide), BF16),
            pltpu.VMEM((2 * channels, (rows + 2) * wide), BF16),
            pltpu.VMEM((3 * channels, rows * wide), BF16),
            pltpu.VMEM((4 * channels, wide), F32),
            pltpu.VMEM((2, rows, channels, wide), F32),
            pltpu.VMEM((rows, channels, wide), BF16),
            pltpu.VMEM((rows, channels, wide), BF16),
            pltpu.VMEM((12, channels, LANES), F32),
            pltpu.VMEM((8, channels, LANES), F32),
            pltpu.VMEM((2 * channels, LANES), F32),
            pltpu.VMEM((2 * channels, LANES), F32),
            pltpu.VMEM((64, 8, channels), F32),
            pltpu.VMEM((total, LANES), BF16),
            pltpu.VMEM((3, inbox[0], LANES), BF16),
            pltpu.VMEM((3, inbox[1], LANES), BF16),
            pltpu.VMEM((3, inbox[2], LANES), BF16),
            pltpu.VMEM((3 * stride[0], LANES), BF16),
            pltpu.VMEM((3 * stride[1], LANES), BF16),
            pltpu.VMEM((total, LANES), BF16),
            pltpu.SemaphoreType.DMA((150,)),
            pltpu.SemaphoreType.DMA((150,)),
            pltpu.SemaphoreType.DMA((16,)),
        ],
        compiler_params=pltpu.CompilerParams(
            collective_id=0, has_side_effects=True, vmem_limit_bytes=60 * 1024 * 1024
        ),
    )(
        turned(latents), turned(hint), turned(cotangent),
        conv_weight[0].transpose(0, 2, 1).reshape(3, 3 * channels, 2 * channels), ctrl_weight[0],
        norm_gain, norm_bias,
    )
    acts, conv, ctrl, gain, bias = pl.pallas_call(
        functools.partial(deliver, channels),
        out_shape=(
            jax.ShapeDtypeStruct((samples, rows, channels, cols), BF16),
            jax.ShapeDtypeStruct((9 * channels, 2 * channels), BF16),
            jax.ShapeDtypeStruct((channels, channels), F32),
            jax.ShapeDtypeStruct((1, 2 * channels), F32),
            jax.ShapeDtypeStruct((1, 2 * channels), F32),
        ),
        in_specs=[vmem] * 4,
        out_specs=(anywhere, anywhere, vmem, vmem, vmem),
        scratch_shapes=[
            pltpu.VMEM((3 * channels, LANES), BF16),
            pltpu.SemaphoreType.DMA((20,)),
        ],
        compiler_params=pltpu.CompilerParams(vmem_limit_bytes=24 * 1024 * 1024),
    )(*out)
    return (
        acts.reshape(1, samples, frames, rows, channels, cols).transpose(0, 1, 2, 3, 5, 4),
        conv.reshape(1, 9, channels, 2 * channels).transpose(0, 1, 3, 2),
        ctrl[None],
        gain,
        bias,
    )


def grid_of(mesh):
    space = mesh.shape["space"]
    columns = 4 if space >= 32 else 2
    return (space // columns, columns, mesh.shape["dp"])


def solution(mesh):
    return jax.shard_map(
        functools.partial(on_device, grid_of(mesh)),
        mesh=mesh,
        in_specs=(
            P("dp", None, "space", None, None),
            P("dp", None, "space", None, None),
            P("dp", None, "space", None, None),
            P("segment", None, None, None),
            P("segment", None, None),
            P("segment", None),
            P("segment", None),
        ),
        out_specs=(
            P("segment", "dp", None, "space", None, None),
            P("segment", None, None, None),
            P("segment", None, None),
            P("segment", None),
            P("segment", None),
        ),
        check_vma=False,
    )
```

```python
import functools

import jax
import jax.numpy as jnp
from jax import lax
from jax.experimental import pallas as pl
from jax.experimental.pallas import tpu as pltpu
from jax.sharding import PartitionSpec as P

MESH = pl.DeviceIdType.MESH
F32 = jnp.float32
BF16 = jnp.bfloat16
EPS = 1e-05
GROUPS = 32
LANES = 128
UNIT = 2048
CHUNK = 32
HIGH = lax.Precision.HIGHEST

ORDERS = (("x", "y", "z"), ("y", "x", "z"), ("z", "x", "y"))
PARTS = {1: ((0, 2 * UNIT), (1, 2 * UNIT), (2, UNIT)), 2: ((0, 3 * UNIT), (1, 3 * UNIT), (2, 2 * UNIT))}


def nt_dot(a, b, precision=None):
    return lax.dot_general(
        a, b, (((1,), (1,)), ((), ())), precision=precision, preferred_element_type=F32
    )


def tn_dot(a, b, precision=None):
    return lax.dot_general(
        a, b, (((0,), (0,)), ((), ())), precision=precision, preferred_element_type=F32
    )


def nn_dot(a, b):
    return jnp.dot(a, b, preferred_element_type=F32)


def sigmoid(v):
    return 1.0 / (1.0 + jnp.exp(-v))


def part_rows(size, halves, p):
    rows, out = PARTS[halves][p][1], []
    for axis in ORDERS[PARTS[halves][p][0]]:
        rows //= size[axis]
        out.append(rows)
    return tuple(out)


def largest(size, value):
    return [
        max(value(part_rows(size, halves, p), ORDERS[PARTS[halves][p][0]], stage) for halves in (1, 2) for p in range(3))
        for stage in range(3)
    ]


class Slots:
    def __init__(self):
        self.index = {}

    def __call__(self, name):
        return self.index.setdefault(name, len(self.index))


class Names(Slots):
    def __init__(self):
        super().__init__()
        self.local = Slots()
        self.boxes = {}

    def box(self, name, count):
        return self.boxes.setdefault(name, (sum(n for _, n in self.boxes.values()), count))[0]


def body(
    dims,
    slots,
    lat_hbm, hint_hbm, cot_hbm, w_hbm, cw_hbm, gain_ref, bias_ref,
    acts_hbm, grads_hbm, gain_out, bias_out,
    x_ext, g_ext, hint_v, w_v, cw_v, wb, act, act_t, g3, y, dact, out_v, last_v,
    columns, sums_v, gain_c, bias_c,
    s_recv, grads, r1, r2, r3, s1, s2, gathered,
    send_sem, recv_sem, local_sem,
):
    NZ, NX, NY, samples, rows, channels = dims
    cells = rows * LANES
    wide = samples * LANES
    space_count = NZ * NX
    seg = lax.axis_index("segment")
    space = lax.axis_index("space")
    dp = lax.axis_index("dp")
    zi = space // NX
    xi = lax.rem(space, NX)
    other = 1 - seg
    up = lax.rem(space + space_count - 1, space_count)
    down = lax.rem(space + 1, space_count)
    size = {"x": NX, "y": NY, "z": NZ}
    mine = {"x": xi, "y": dp, "z": zi}

    def peer(axis, k, core=None):
        if axis == "x":
            place = {"space": zi * NX + lax.rem(xi + k, NX), "dp": dp}
        elif axis == "z":
            place = {"space": lax.rem(zi + k, NZ) * NX + xi, "dp": dp}
        else:
            place = {"space": space, "dp": lax.rem(dp + k, NY)}
        place["segment"] = seg if core is None else core
        return place

    def at(space_id, core):
        return {"space": space_id, "dp": dp, "segment": core}

    def send(name, src, dst, place):
        slot = slots(name)
        return pltpu.make_async_remote_copy(
            src_ref=src, dst_ref=dst, send_sem=send_sem.at[slot], recv_sem=recv_sem.at[slot],
            device_id=(place["segment"], place["space"], place["dp"]), device_id_type=MESH,
        )

    def local(name, src, dst):
        return pltpu.make_async_copy(src, dst, local_sem.at[slots.local(name)])

    def start(copies):
        for c in copies:
            c.start()

    def wait(copies):
        for c in copies:
            c.wait()

    inner = pl.ds(1, rows)

    def sample(b):
        return pl.ds(b * LANES, LANES)

    def loads(is_encoder, key):
        if key == "weight":
            return [local(key, w_hbm, w_v)]
        if key == "control":
            return [local(key, cw_hbm, cw_v)]
        if key == "hint":
            return [local(f"{key} {b}", hint_hbm.at[b], hint_v.at[:, :, sample(b)]) for b in range(samples)]
        source, target = (lat_hbm, x_ext) if is_encoder else (cot_hbm, g_ext)
        return [local(f"{key} {b}", source.at[b], target.at[inner, :, sample(b)]) for b in range(samples)]

    @pl.when(seg == 0)
    def _():
        for key in ("main", "weight", "control", "hint"):
            start(loads(True, key))

    @pl.when(seg == 1)
    def _():
        for key in ("main", "weight", "hint", "control"):
            start(loads(False, key))

    barrier = pltpu.get_barrier_semaphore()
    places = [peer("x", k) for k in range(1, NX)]
    places += [peer("y", k) for k in range(1, NY)]
    places += [peer("z", k) for k in range(1, NZ)]
    places += [peer("z", k, other) for k in range(NZ)]
    places += [at(n, c) for n in (up, down) for c in (seg, other)]
    for place in places:
        pl.semaphore_signal(
            barrier, inc=1,
            device_id=(place["segment"], place["space"], place["dp"]), device_id_type=MESH,
        )

    line = lax.broadcasted_iota(jnp.int32, (8, LANES), 0)
    ones = jnp.ones((8, LANES), F32)
    first_lane = jnp.where(lax.broadcasted_iota(jnp.int32, (8, LANES), 1) == 0, 1.0, 0.0)

    def to_row(block, pick=None):
        return nt_dot(ones if pick is None else pick, block, HIGH)[0:1, :]

    def to_column(value, k):
        return tn_dot(value, jnp.where(line == k, 1.0, 0.0), HIGH)

    def eight(parts):
        count = sum(p.shape[0] for p in parts)
        if count < 8:
            parts = parts + [jnp.zeros((8 - count, parts[0].shape[1]), F32)]
        return jnp.concatenate(parts, axis=0)

    gain_c[...] = to_column(eight([gain_ref[...]]), 0)
    bias_c[...] = to_column(eight([bias_ref[...]]), 0)

    lane = lax.broadcasted_iota(jnp.int32, (channels, channels), 0).astype(F32)
    lane_t = lax.broadcasted_iota(jnp.int32, (channels, channels), 1).astype(F32)

    def group_mean(values, width):
        same = jnp.floor((lane + 0.5) / width) == jnp.floor((lane_t + 0.5) / width)
        return jnp.dot(
            values, jnp.where(same, 1.0, 0.0), precision=HIGH, preferred_element_type=F32
        ) / width

    def edges(name, ref, src, core):
        return [
            send(name + " down", src[1], ref.at[0], at(down, core)),
            send(name + " up", src[0], ref.at[rows + 1], at(up, core)),
        ]

    def zero_outside(ref):
        blank = jnp.zeros(ref.shape[1:], ref.dtype)

        @pl.when(space == 0)
        def _():
            ref[0] = blank

        @pl.when(space == space_count - 1)
        def _():
            ref[rows + 1] = blank

    def chunks(step, width=CHUNK):
        def run(i, carry):
            step(pl.multiple_of(i * width, width))
            return carry
        lax.fori_loop(0, channels // width, run, 0)

    def local_stats(ref, base, name):
        def step(at_row):
            where = pl.ds(at_row, CHUNK)
            for b in range(samples):
                v = [ref[base + r, where, sample(b)].astype(F32) for r in range(rows)]
                mean = jnp.sum(sum(v), axis=1, keepdims=True) / cells
                sums_v[b, where, :] = jnp.broadcast_to(mean, (CHUNK, LANES))
                sums_v[samples + b, where, :] = sum(jnp.square(t - mean) for t in v)
        chunks(step)
        lines = [to_row(sums_v[b], first_lane) for b in range(samples)]
        lines += [to_row(sums_v[samples + b]) for b in range(samples)]
        put(name, "x", eight(lines))

    def put(name, axis, value):
        s_recv[slots.box(name, size[axis]) + mine[axis]] = value

    def exchange(name, axis, core=None, landing=False):
        base = slots.box(name, size[axis])
        copies = []
        for k in range(0 if core is not None else 1, size[axis]):
            owner = lax.rem(mine[axis] + size[axis] - k, size[axis]) if landing else mine[axis]
            copies.append(send(f"{name} {k}", s_recv.at[base + mine[axis]], s_recv.at[base + owner], peer(axis, k, core)))
        return copies

    def arrivals(name, axis):
        base = slots.box(name, size[axis])
        return [s_recv.at[base + k] for k in range(size[axis])]

    def small_wait(name, axis):
        wait(exchange(name, axis, landing=True))

    def merge(refs, count):
        mean = sum(r[0:samples, :] for r in refs) / len(refs)
        spread = sum(r[samples:2 * samples, :] for r in refs)
        apart = sum(jnp.square(r[0:samples, :] - mean) for r in refs)
        return mean, spread + count * apart

    def finish_stats(mean, spread, width):
        total = cells * space_count
        padded = eight([mean])
        middle = group_mean(padded, width)
        offset = padded - middle
        var = group_mean(eight([spread]) / total + offset * offset, width)
        scale = lax.rsqrt(var + EPS)
        for b in range(samples):
            columns[b] = to_column(middle, b)
            columns[samples + b] = to_column(scale, b)

    def activate(halves):
        for h in halves:
            def step(at_row):
                where = pl.ds(at_row, CHUNK)
                inside = pl.ds(pl.multiple_of(at_row + h * channels, CHUNK), CHUNK)
                gain, bias = gain_c[inside, :], bias_c[inside, :]
                for b in range(samples):
                    middle, rate = columns[b, where, :], columns[samples + b, where, :]
                    for r in range(rows + 2):
                        xhat = (x_ext[r, where, sample(b)].astype(F32) - middle) * rate
                        u = xhat * gain + bias
                        a = (u * sigmoid(u)).astype(BF16)
                        act[r, inside, sample(b)] = a
                        act_t[inside, pl.ds(r * wide + b * LANES, LANES)] = a
            chunks(step)
        blank = jnp.zeros((2 * channels, wide), BF16)
        for r, edge in ((0, 0), (rows + 1, space_count - 1)):
            @pl.when(space == edge)
            def _():
                act[r] = blank
                act_t[:, r * wide:(r + 1) * wide] = blank

    lanes = lax.broadcasted_iota(jnp.int32, (channels, LANES), 1)

    def shift(v, step):
        column = 0 if step == 1 else LANES - 1
        return jnp.where(lanes[:v.shape[0]] != column, pltpu.roll(v, step % LANES, axis=1), 0.0)

    def forward(halves, target):
        width = channels * len(halves)

        def step(r, carry):
            total = None
            for dr in range(3):
                part = nn_dot(w_v[dr, :, 0:width], act[r + dr, 0:width, :])
                total = part if total is None else total + part
            y[0:3 * channels, :] = total
            y[3 * channels:4 * channels, :] = tn_dot(cw_v[...], hint_v[r])
            for b in range(samples):
                def tap(dc):
                    return y[dc * channels:(dc + 1) * channels, sample(b)]
                total = tap(1) + tap(3) + shift(tap(0), 1) + shift(tap(2), -1)
                x = x_ext[r + 1, :, sample(b)].astype(F32)
                target[r, :, sample(b)] = (x + total).astype(BF16)
            return carry
        lax.fori_loop(0, rows, step, 0)

    def turn_weights(halves):
        count = -(-channels * len(halves) // LANES)
        for dc in range(3):
            def block(j, carry):
                where = pl.ds(pl.multiple_of(j * LANES, LANES), LANES)
                taps = [w_v[2 - d, dc * channels:(dc + 1) * channels, where] for d in range(3)]
                wb[dc, where, :] = jnp.concatenate(taps, axis=0).T
                return carry
            lax.fori_loop(0, count, block, 0)

    def transposed(halves):
        def step(r, carry):
            g = g_ext[pl.ds(r, 3)].reshape(3 * channels, wide)
            for h in halves:
                for dc in range(3):
                    y[dc * channels:(dc + 1) * channels, :] = nn_dot(wb[dc, h * channels:(h + 1) * channels, :], g)
                for b in range(samples):
                    def tap(dc):
                        return y[dc * channels:(dc + 1) * channels, sample(b)]
                    dact[h, r, :, sample(b)] = tap(1) + shift(tap(0), -1) + shift(tap(2), 1)
            return carry
        lax.fori_loop(0, rows, step, 0)

    def shift_gradient():
        def step(r, carry):
            for b in range(samples):
                g = g_ext[r + 1, :, sample(b)]
                where = pl.ds(pl.multiple_of(r * wide + b * LANES, LANES), LANES)
                v = g.astype(F32)
                g3[0:channels, where] = shift(v, -1).astype(BF16)
                g3[channels:2 * channels, where] = g
                g3[2 * channels:3 * channels, where] = shift(v, 1).astype(BF16)
            return carry
        lax.fori_loop(0, rows, step, 0)

    def blocks(value, base):
        count = value.shape[0]
        for j in range(value.shape[1] // LANES):
            grads[base + j * count:base + (j + 1) * count, :] = value[:, j * LANES:(j + 1) * LANES].astype(BF16)

    def control_gradient(base):
        total = None
        for r in range(rows):
            where = pl.ds(r * wide, wide)
            part = nt_dot(hint_v[r], g3[channels:2 * channels, where])
            total = part if total is None else total + part
        blocks(jnp.concatenate([total, jnp.zeros((channels, 3 * LANES - channels), F32)], axis=1), base)

    def kernel_gradient(halves, dr):
        width = 3 * LANES if len(halves) == 1 else 2 * channels
        total = nt_dot(g3[...], act_t[0:width, dr * wide:(dr + rows) * wide])
        blocks(total, dr * 3 * channels * (width // LANES))

    def norm_backward(halves):
        for h in halves:
            def step(at_row):
                where = pl.ds(at_row, CHUNK)
                inside = pl.ds(pl.multiple_of(at_row + h * channels, CHUNK), CHUNK)
                gain, bias = gain_c[inside, :], bias_c[inside, :]
                for b in range(samples):
                    middle, rate = columns[b, where, :], columns[samples + b, where, :]
                    first = second = None
                    for r in range(rows):
                        xhat = (x_ext[r + 1, where, sample(b)].astype(F32) - middle) * rate
                        u = xhat * gain + bias
                        s = sigmoid(u)
                        du = dact[h, r, where, sample(b)] * s * (1.0 + u * (1.0 - s))
                        dact[h, r, where, sample(b)] = du
                        first = du if first is None else first + du
                        second = du * xhat if second is None else second + du * xhat
                    sums_v[4 * h + b, where, :] = first
                    sums_v[4 * h + samples + b, where, :] = second
            chunks(step)
        return eight([to_row(sums_v[k]) for k in range(4 * len(halves))])

    stride = tuple(largest(size, lambda ns, axes, stage: ns[stage]))

    def part_geometry(p, halves):
        parts = PARTS[halves]
        base = sum(n for _, n in parts[:p])
        return ORDERS[parts[p][0]], part_rows(size, halves, p), base

    def stage_base(p, halves, stage):
        base = part_geometry(p, halves)[2]
        return base if stage == 0 else p * stride[stage - 1]

    def scatter_copies(p, halves, stage):
        axes, ns, _ = part_geometry(p, halves)
        axis, n = axes[stage], ns[stage]
        src = (grads, s1, s2)[stage]
        dst = (r1, r2, r3)[stage]
        base = stage_base(p, halves, stage)
        copies = []
        for k in range(1, size[axis]):
            to = lax.rem(mine[axis] + k, size[axis])
            where = pl.ds(pl.multiple_of(base + to * n, 16), n)
            inbox = dst.at[p, pl.ds((k - 1) * n, n), :]
            copies.append(send(f"rs {p} {stage} {k}", src.at[where, :], inbox, peer(axis, k)))
        return copies

    def scatter_sum(p, halves, stage):
        axes, ns, part_base = part_geometry(p, halves)
        axis, n = axes[stage], ns[stage]
        src = (grads, s1, s2)[stage]
        inbox = (r1, r2, r3)[stage]
        own = stage_base(p, halves, stage) + mine[axis] * n
        if stage == 0:
            dst, to = s1, p * stride[0]
        elif stage == 1:
            dst, to = s2, p * stride[1]
        else:
            dst, to = gathered, part_base + sum(mine[a] * m for a, m in zip(axes, ns))
        chunk = 64 if n % 64 == 0 else 16

        def step(i, carry):
            total = src[pl.ds(pl.multiple_of(own + i * chunk, 16), chunk), :].astype(F32)
            for k in range(size[axis] - 1):
                total += inbox[p, pl.ds(pl.multiple_of(k * n + i * chunk, 16), chunk), :].astype(F32)
            dst[pl.ds(pl.multiple_of(to + i * chunk, 16), chunk), :] = total.astype(BF16)
            return carry
        lax.fori_loop(0, n // chunk, step, 0)

    def gather_copies(p, halves, stage):
        axes, ns, part_base = part_geometry(p, halves)
        axis, n = axes[stage], ns[stage]
        offset = part_base + sum(mine[a] * m for a, m in zip(axes[:stage + 1], ns[:stage + 1]))
        where = pl.ds(pl.multiple_of(offset, 16), n)
        return [
            send(f"ag {p} {stage} {k}", gathered.at[where, :], gathered.at[where, :], peer(axis, k))
            for k in range(1, size[axis])
        ]

    def gather_wait(p, halves, stage):
        axes, ns, part_base = part_geometry(p, halves)
        axis, n = axes[stage], ns[stage]
        base = part_base + sum(mine[a] * m for a, m in zip(axes[:stage], ns[:stage]))
        for k in range(1, size[axis]):
            source = lax.rem(mine[axis] + size[axis] - k, size[axis])
            where = pl.ds(pl.multiple_of(base + source * n, 16), n)
            send(f"ag {p} {stage} {k}", gathered.at[where, :], gathered.at[where, :], peer(axis, k)).wait()

    def reduce_rest(halves, name, axes, value):
        def small_start(stage):
            put(f"{name} {stage}", axes[stage], value)
            start(exchange(f"{name} {stage}", axes[stage]))

        turn = (0, 1, 2) if halves == 1 else (1, 0, 2)
        small_start(0)
        for stage in range(3):
            for p in turn:
                wait(scatter_copies(p, halves, stage))
                scatter_sum(p, halves, stage)
                start(scatter_copies(p, halves, stage + 1) if stage < 2 else gather_copies(p, halves, 2))
            if stage < len(axes):
                small_wait(f"{name} {stage}", axes[stage])
                value = sum(r[...] for r in arrivals(f"{name} {stage}", axes[stage]))
                if stage + 1 < len(axes):
                    small_start(stage + 1)
        for stage in (2, 1, 0):
            for p in turn:
                gather_wait(p, halves, stage)
                if stage > 0:
                    start(gather_copies(p, halves, stage - 1))
                else:
                    start([part_out(p, halves)])
        return value

    def part_out(p, halves):
        base, n = part_geometry(p, halves)[2], PARTS[halves][p][1]
        return local(f"part {p}", gathered.at[pl.ds(base, n), :], grads_hbm.at[pl.ds(base, n), :])

    def saves(source):
        return [local(f"acts {b}", source.at[:, :, sample(b)], acts_hbm.at[b]) for b in range(samples)]

    def clear_tail(halves):
        used = 3 * 3 * channels * (3 if halves == 1 else 5) + 3 * channels
        total = sum(n for _, n in PARTS[halves])
        grads[used:total, :] = jnp.zeros((total - used, LANES), BF16)

    @pl.when(seg == 0)
    def _():
        wait(loads(True, "main"))
        local_stats(x_ext, 1, "a x")

    @pl.when(seg == 1)
    def _():
        wait(loads(False, "main"))
        clear_tail(2)
        shift_gradient()

    pl.semaphore_wait(barrier, len(places))

    @pl.when(seg == 0)
    def _encoder():
        halves = (0,)
        start(exchange("a x", "x"))
        halo = edges("lat", x_ext, (x_ext.at[1], x_ext.at[rows]), 0)
        start(halo)
        act_t[channels:3 * LANES, :] = jnp.zeros((3 * LANES - channels, act_t.shape[1]), BF16)
        clear_tail(1)
        small_wait("a x", "x")
        mean, spread = merge(arrivals("a x", "x"), float(cells))
        put("a z", "z", eight([mean, spread]))
        start(exchange("a z", "z"))
        wait(loads(True, "weight"))
        turn_weights(halves)
        small_wait("a z", "z")
        mean, spread = merge(arrivals("a z", "z"), float(cells * NX))
        finish_stats(mean, spread, channels // GROUPS)
        wait(halo)
        activate(halves)
        wait(loads(True, "hint"))
        wait(loads(True, "control"))
        forward(halves, out_v)
        ahead = [send("o", out_v, x_ext.at[inner], at(space, 1))]
        start(ahead)
        start(saves(out_v))
        local_stats(out_v, 0, "b x")
        start(exchange("b x", "x"))
        small_wait("b x", "x")
        mean, spread = merge(arrivals("b x", "x"), float(cells))
        put("b z", "z", eight([mean, spread]))
        stats = exchange("b z", "z", core=1)
        start(stats)
        halo = edges("o", x_ext, (out_v.at[0], out_v.at[rows - 1]), 1)
        start(halo)
        ahead += halo
        for c in ahead + stats:
            c.wait_send()
        wait(saves(out_v))
        send("g", out_v, g_ext.at[inner], at(space, 0)).wait_recv()
        shift_gradient()
        kernel_gradient(halves, 0)
        kernel_gradient(halves, 1)
        start(scatter_copies(0, 1, 0))
        kernel_gradient(halves, 2)
        start(scatter_copies(1, 1, 0))
        control_gradient(3 * 3 * channels * 3)
        start(scatter_copies(2, 1, 0))
        for c in edges("g", g_ext, (out_v.at[0], out_v.at[rows - 1]), 0):
            c.wait_recv()
        zero_outside(g_ext)
        transposed(halves)
        sums = norm_backward(halves)
        sums = reduce_rest(1, "e", ("x", "z", "y"), sums)
        blank = jnp.zeros((1, channels), F32)
        bias_out[...] = jnp.concatenate([sums[0:1] + sums[1:2], blank], axis=1)
        gain_out[...] = jnp.concatenate([sums[2:3] + sums[3:4], blank], axis=1)
        wait([part_out(p, len(halves)) for p in range(3)])

    @pl.when(seg == 1)
    def _decoder():
        halves = (0, 1)
        halo = edges("cot", g_ext, (g_ext.at[1], g_ext.at[rows]), 1)
        start(halo)
        wait(loads(False, "weight"))
        turn_weights(halves)
        wait(halo)
        zero_outside(g_ext)
        transposed(halves)
        wait(loads(False, "hint"))
        control_gradient(3 * 3 * channels * 5)
        wait(loads(False, "control"))
        send("o", out_v, x_ext.at[inner], at(space, 1)).wait_recv()
        for c in exchange("b z", "z", core=1, landing=True):
            c.wait_recv()
        mean, spread = merge(arrivals("b z", "z"), float(cells * NX))
        width = 2 * channels // GROUPS
        finish_stats(mean, spread, width)
        sums = norm_backward(halves)
        put("c x", "x", sums)
        start(exchange("c x", "x"))
        for c in edges("o", x_ext, (out_v.at[0], out_v.at[rows - 1]), 1):
            c.wait_recv()
        activate(halves)
        small_wait("c x", "x")
        sums = sum(r[...] for r in arrivals("c x", "x"))
        put("c z", "z", sums)
        start(exchange("c z", "z"))
        for dr in range(3):
            kernel_gradient(halves, dr)
        start(scatter_copies(1, 2, 0))
        small_wait("c z", "z")
        start(scatter_copies(2, 2, 0))
        sums = sum(r[...] for r in arrivals("c z", "z"))
        total = float(cells * space_count)
        for h in halves:
            gain = gain_ref[:, h * channels:(h + 1) * channels]
            means = group_mean(sums * gain, width) / total
            for k in range(4):
                columns[4 + 4 * h + k] = to_column(means, 4 * h + k)

        def step(at_row):
            where = pl.ds(at_row, CHUNK)
            gains = [gain_c[pl.ds(pl.multiple_of(at_row + h * channels, CHUNK), CHUNK), :] for h in halves]
            for b in range(samples):
                middle, rate = columns[b, where, :], columns[samples + b, where, :]
                means = [(columns[4 + 4 * h + b, where, :], columns[6 + 4 * h + b, where, :]) for h in halves]
                for r in range(rows):
                    xhat = (x_ext[r + 1, where, sample(b)].astype(F32) - middle) * rate
                    dj = []
                    for h in halves:
                        dx = dact[h, r, where, sample(b)] * gains[h]
                        dj.append((dx - means[h][0] - xhat * means[h][1]) * rate)
                    dh = (g_ext[r + 1, where, sample(b)].astype(F32) + dj[0]).astype(BF16)
                    dskip = dj[1].astype(BF16)
                    out_v[r, where, sample(b)] = (dh.astype(F32) + dskip.astype(F32)).astype(BF16)
        chunks(step)
        back = [send("g", out_v, g_ext.at[inner], at(space, 0))]
        back += edges("g", g_ext, (out_v.at[0], out_v.at[rows - 1]), 0)
        start(back)
        start(scatter_copies(0, 2, 0))
        forward(halves, last_v)
        start(saves(last_v))
        sums = reduce_rest(2, "f", ("y",), sums)
        bias_out[...] = jnp.concatenate([sums[0:1] + sums[1:2], sums[4:5] + sums[5:6]], axis=1)
        gain_out[...] = jnp.concatenate([sums[2:3] + sums[3:4], sums[6:7] + sums[7:8]], axis=1)
        wait([part_out(p, len(halves)) for p in range(3)])
        wait(saves(last_v))
        for c in back:
            c.wait_send()


def deliver(
    channels, acts_in, grads_in, gain_in, bias_in,
    acts_out, conv_out, ctrl_out, gain_out, bias_out,
    acts_v, grads_v, ctrl_v, gain_v, bias_v, zeros_v, load_sem, save_sem,
):
    seg = lax.axis_index("segment")
    high = 3 * channels

    def run(count):
        base, last = 3 * count * high, channels - 2 * LANES
        moves = [(grads_in.at[pl.ds(base, high), :], grads_v.at[pl.ds(base, high), :], None)]
        for b in range(acts_v.shape[0]):
            moves.append((acts_in.at[b], acts_v.at[b], acts_out.at[b]))
        for dr in range(3):
            for k in range(count):
                where = pl.ds((dr * count + k) * high, high)
                target = conv_out.at[pl.ds(dr * high, high), pl.ds(k * LANES, LANES)]
                moves.append((grads_in.at[where, :], grads_v.at[where, :], target))
        moves.append((gain_in, gain_v, gain_out))
        moves.append((bias_in, bias_v, bias_out))
        loads = [pltpu.make_async_copy(src, mid, load_sem.at[n]) for n, (src, mid, _) in enumerate(moves)]
        for c in loads:
            c.start()
        saves = []
        if count < 5:
            zeros_v[...] = jnp.zeros(zeros_v.shape, BF16)
            for dr in range(3):
                for k in range(count, 5):
                    target = conv_out.at[pl.ds(dr * high, high), pl.ds(k * LANES, LANES)]
                    saves.append(pltpu.make_async_copy(zeros_v, target, save_sem.at[20 + 2 * dr + k - count]))
            for c in saves:
                c.start()
        for n, (_, mid, target) in enumerate(moves):
            loads[n].wait()
            if target is None:
                ctrl_v[:, 0:LANES] = grads_v[base:base + channels, :].astype(F32)
                ctrl_v[:, LANES:2 * LANES] = grads_v[base + channels:base + 2 * channels, :].astype(F32)
                ctrl_v[:, 2 * LANES:channels] = grads_v[base + 2 * channels:base + high, 0:last].astype(F32)
                save = pltpu.make_async_copy(ctrl_v, ctrl_out, save_sem.at[n])
            else:
                save = pltpu.make_async_copy(mid, target, save_sem.at[n])
            save.start()
            saves.append(save)
        for c in saves:
            c.wait()

    @pl.when(seg == 0)
    def _():
        run(3)

    @pl.when(seg == 1)
    def _():
        run(5)


def on_device(grid, latents, hint, cotangent, conv_weight, ctrl_weight, norm_gain, norm_bias):
    NZ, NX, NY = grid
    samples, frames, rows, cols, channels = latents.shape
    cells = rows * cols
    wide = samples * cols
    dims = (NZ, NX, NY, samples, rows, channels)
    turned = lambda a: a.transpose(0, 1, 2, 4, 3).reshape(samples, rows, channels, cols)
    vmem = pl.BlockSpec(memory_space=pltpu.VMEM)
    anywhere = pl.BlockSpec(memory_space=pl.ANY)
    size = {"x": NX, "y": NY, "z": NZ}
    stride = largest(size, lambda ns, axes, stage: ns[stage])
    inbox = largest(size, lambda ns, axes, stage: ns[stage] * (size[axes[stage]] - 1))
    total = max(sum(n for _, n in parts) for parts in PARTS.values())
    out = pl.pallas_call(
        functools.partial(body, dims, Names()),
        out_shape=(
            jax.ShapeDtypeStruct((samples, rows, channels, cols), BF16),
            jax.ShapeDtypeStruct((total, LANES), BF16),
            jax.ShapeDtypeStruct((1, 2 * channels), F32),
            jax.ShapeDtypeStruct((1, 2 * channels), F32),
        ),
        in_specs=[anywhere] * 5 + [vmem] * 2,
        out_specs=(anywhere, anywhere, vmem, vmem),
        scratch_shapes=[
            pltpu.VMEM((rows + 2, channels, wide), BF16),
            pltpu.VMEM((rows + 2, channels, wide), BF16),
            pltpu.VMEM((rows, channels, wide), BF16),
            pltpu.VMEM((3, 3 * channels, 2 * channels), BF16),
            pltpu.VMEM((channels, channels), BF16),
            pltpu.VMEM((3, 2 * channels, 3 * channels), BF16),
            pltpu.VMEM((rows + 2, 2 * channels, wide), BF16),
            pltpu.VMEM((2 * channels, (rows + 2) * wide), BF16),
            pltpu.VMEM((3 * channels, rows * wide), BF16),
            pltpu.VMEM((4 * channels, wide), F32),
            pltpu.VMEM((2, rows, channels, wide), F32),
            pltpu.VMEM((rows, channels, wide), BF16),
            pltpu.VMEM((rows, channels, wide), BF16),
            pltpu.VMEM((12, channels, LANES), F32),
            pltpu.VMEM((8, channels, LANES), F32),
            pltpu.VMEM((2 * channels, LANES), F32),
            pltpu.VMEM((2 * channels, LANES), F32),
            pltpu.VMEM((64, 8, channels), F32),
            pltpu.VMEM((total, LANES), BF16),
            pltpu.VMEM((3, inbox[0], LANES), BF16),
            pltpu.VMEM((3, inbox[1], LANES), BF16),
            pltpu.VMEM((3, inbox[2], LANES), BF16),
            pltpu.VMEM((3 * stride[0], LANES), BF16),
            pltpu.VMEM((3 * stride[1], LANES), BF16),
            pltpu.VMEM((total, LANES), BF16),
            pltpu.SemaphoreType.DMA((150,)),
            pltpu.SemaphoreType.DMA((150,)),
            pltpu.SemaphoreType.DMA((16,)),
        ],
        compiler_params=pltpu.CompilerParams(
            collective_id=0, has_side_effects=True, vmem_limit_bytes=60 * 1024 * 1024
        ),
    )(
        turned(latents), turned(hint), turned(cotangent),
        conv_weight[0].transpose(0, 2, 1).reshape(3, 3 * channels, 2 * channels), ctrl_weight[0],
        norm_gain, norm_bias,
    )
    acts, conv, ctrl, gain, bias = pl.pallas_call(
        functools.partial(deliver, channels),
        out_shape=(
            jax.ShapeDtypeStruct((samples, rows, channels, cols), BF16),
            jax.ShapeDtypeStruct((9 * channels, 2 * channels), BF16),
            jax.ShapeDtypeStruct((channels, channels), F32),
            jax.ShapeDtypeStruct((1, 2 * channels), F32),
            jax.ShapeDtypeStruct((1, 2 * channels), F32),
        ),
        in_specs=[anywhere] * 4,
        out_specs=(anywhere,) * 5,
        scratch_shapes=[
            pltpu.VMEM((samples, rows, channels, cols), BF16),
            pltpu.VMEM((total, LANES), BF16),
            pltpu.VMEM((channels, channels), F32),
            pltpu.VMEM((1, 2 * channels), F32),
            pltpu.VMEM((1, 2 * channels), F32),
            pltpu.VMEM((3 * channels, LANES), BF16),
            pltpu.SemaphoreType.DMA((20,)),
            pltpu.SemaphoreType.DMA((26,)),
        ],
        compiler_params=pltpu.CompilerParams(vmem_limit_bytes=60 * 1024 * 1024),
    )(*out)
    return (
        acts.reshape(1, samples, frames, rows, channels, cols).transpose(0, 1, 2, 3, 5, 4),
        conv.reshape(1, 9, channels, 2 * channels).transpose(0, 1, 3, 2),
        ctrl[None],
        gain,
        bias,
    )


def grid_of(mesh):
    space = mesh.shape["space"]
    columns = 4 if space >= 32 else 2
    return (space // columns, columns, mesh.shape["dp"])


def solution(mesh):
    return jax.shard_map(
        functools.partial(on_device, grid_of(mesh)),
        mesh=mesh,
        in_specs=(
            P("dp", None, "space", None, None),
            P("dp", None, "space", None, None),
            P("dp", None, "space", None, None),
            P("segment", None, None, None),
            P("segment", None, None),
            P("segment", None),
            P("segment", None),
        ),
        out_specs=(
            P("segment", "dp", None, "space", None, None),
            P("segment", None, None, None),
            P("segment", None, None),
            P("segment", None),
            P("segment", None),
        ),
        check_vma=False,
    )
```
